256 devices in a mesh: dp: 2 (over core), row: 16 (over y, x), col: 8 (over z).
Axes of the slice: x: 4, y: 4, z: 8, core: 2. Of those that a mesh axis runs over, the one named last changes fastest.
Arguments:
- ffn_input: bfloat16 [2, 1280, 4096], P('dp', None, 'row'), may hold values from -6 to 6
- gate_act: bfloat16 [2, 1280, 14336], P('dp', 'row', 'col'), may hold values from -8 to 8
- up_act: bfloat16 [2, 1280, 14336], P('dp', 'row', 'col'), may hold values from -6 to 6
- hidden_grad: bfloat16 [2, 1280, 14336], P('dp', 'row', 'col'), may hold values from -0.29882812 to 0.29882812
- stream_grad: bfloat16 [2, 1280, 4096], P('dp', None, 'row'), may hold values from -0.29882812 to 0.29882812
- w_gate: bfloat16 [4096, 14336], P('row', 'col'), may hold values from -0.09375 to 0.09375
- w_up: bfloat16 [4096, 14336], P('row', 'col'), may hold values from -0.09375 to 0.09375
- gate_keep: int32 [32, 112], P('row', 'col'), may hold values 0 or 1
- up_keep: int32 [32, 112], P('row', 'col'), may hold values 0 or 1
- w_out: bfloat16 [8192, 4096], P('col', 'row'), may hold values from -0.0625 to 0.0625
- queries: bfloat16 [2, 1280, 8192], P('dp', 'row', 'col'), may hold values from -6 to 6
- keys: bfloat16 [2, 1280, 1024], P('dp', 'row', 'col'), may hold values from -6 to 6
- values: bfloat16 [2, 1280, 1024], P('dp', 'row', 'col'), may hold values from -6 to 6
Outputs:
- grad_w_gate: bfloat16 [4096, 14336], P('row', 'col')
- grad_w_up: bfloat16 [4096, 14336], P('row', 'col')
- query_grad: bfloat16 [2, 1280, 8192], P('dp', 'row', 'col')
- key_grad: bfloat16 [2, 1280, 1024], P('dp', 'row', 'col')
- value_grad: bfloat16 [2, 1280, 1024], P('dp', 'row', 'col')
The draws below stay inside these ranges and needn't reach their ends.
Inputs may be any that keep to these rules, and one draw needn't show every extreme that they name: `gate_keep`: 1 marks a trained 128 x 128 block. `up_keep`: 1 marks a trained 128 x 128 block.
All inputs are finite; a program needn't handle non-finite values.
Results may differ from the reference program's by a relative error of at most 0.039.
Values may be sent and summed in bfloat16 or wider, within the bound.
A program may use at most 128 MiB of HBM per device.

```python
import math
import jax
import jax.numpy as jnp
from jax import lax

D = 4096
FF = 14336
HEADS = 64
KV_HEADS = 8
HEAD_DIM = 128
BLOCK = 128
SEQ = 1280
SEQS = 2
GROUP = 8


def draw_queries(key, part):
    key = jax.random.fold_in(key, 5)
    result = jnp.clip(jax.random.normal(key, (SEQS, SEQ, HEADS * HEAD_DIM), jnp.float32), -6.0, 6.0)
    return result.astype(jnp.bfloat16)


def draw_keys(key, part):
    key = jax.random.fold_in(key, 7)
    result = jnp.clip(jax.random.normal(key, (SEQS, SEQ, KV_HEADS * HEAD_DIM), jnp.float32), -6.0, 6.0)
    return result.astype(jnp.bfloat16)


def set_ends(values, key, least, top_value):
    longest = values.shape.index(max(values.shape))
    spots = []
    for shift in (0, 1):
        where = [jax.random.randint(jax.random.fold_in(key, axis), (), 0, length) for axis, length in enumerate(values.shape)]
        where[longest] = (where[longest] + shift) % values.shape[longest]
        spots.append(tuple(where))
    return values.at[spots[0]].set(least).at[spots[1]].set(top_value)


def steps_of(key, shape, cuts, smallest, top_value):
    def one(dim, blocks):
        draws = jax.random.uniform(jax.random.fold_in(jax.random.fold_in(key, 6), dim), (blocks,), jnp.float32, smallest / len(cuts), top_value / len(cuts))
        return jnp.repeat(jnp.exp(draws), shape[dim] // blocks).reshape((-1,) + (1,) * (len(shape) - dim - 1))

    loudness = one(*cuts[0])
    for cut in cuts[1:]:
        loudness = loudness * one(*cut)
    return loudness


def bell_draw(rng, shape, width, bound, shards=(), dtype=jnp.bfloat16):
    values = jax.random.normal(rng, shape, jnp.float32) * width
    if len(shards) > 0:
        values = steps_of(rng, shape, shards, -0.22, 0.18) * values
    return jnp.clip(values, min=-bound, max=bound).astype(dtype)


def setup_inputs(seed: int = 0) -> dict:
    key_list = jax.random.split(jax.random.key(seed), 14)
    ffn_input = bell_draw(key_list[0], (SEQS, SEQ, D), 1.0, 6.0, ((0, 2), (2, 16)))
    gate_act = bell_draw(key_list[1], (SEQS, SEQ, FF), 1.5, 8.0, ((0, 2), (1, 16), (2, 8)))
    up_act = bell_draw(key_list[2], (SEQS, SEQ, FF), 1.0, 6.0, ((0, 2), (1, 16), (2, 8)))
    hidden_grad = bell_draw(key_list[3], (SEQS, SEQ, FF), 0.05, 0.29882812, ((0, 2), (1, 16), (2, 8)))
    stream_grad = bell_draw(key_list[4], (SEQS, SEQ, D), 0.05, 0.29882812, ((0, 2), (2, 16)))
    w_gate = bell_draw(key_list[5], (D, FF), D ** -0.5, 0.09375, ((0, 16), (1, 8)))
    w_up = bell_draw(key_list[6], (D, FF), D ** -0.5, 0.09375, ((0, 16), (1, 8)))
    gate_keep = set_ends((jax.random.randint(key_list[7], (D // BLOCK, FF // BLOCK), 0, 2) < 1).astype(jnp.int32), jax.random.fold_in(key_list[7], 1), 0, 1)
    up_keep = set_ends((jax.random.randint(key_list[8], (D // BLOCK, FF // BLOCK), 0, 2) < 1).astype(jnp.int32), jax.random.fold_in(key_list[8], 1), 0, 1)
    w_out = bell_draw(key_list[9], (HEADS * HEAD_DIM, D), (HEADS * HEAD_DIM) ** -0.5, 0.0625, ((0, 8), (1, 16)))
    queries = draw_queries(jax.random.fold_in(key_list[13], 71), 0)
    keys = draw_keys(jax.random.fold_in(key_list[13], 71), 0)
    values = bell_draw(key_list[12], (SEQS, SEQ, KV_HEADS * HEAD_DIM), 1.0, 6.0, ((0, 2), (1, 16), (2, 8)))
    return dict(ffn_input=ffn_input, gate_act=gate_act, up_act=up_act, hidden_grad=hidden_grad, stream_grad=stream_grad, w_gate=w_gate, w_up=w_up, gate_keep=gate_keep, up_keep=up_keep, w_out=w_out, queries=queries, keys=keys, values=values)


NEGATIVE_FILL = -1e+30

def widened(keep):
    return jnp.repeat(jnp.repeat(keep, BLOCK, axis=0), BLOCK, axis=1).astype(jnp.float32)

def attention_backward(operands):
    query_seq, key_seq, value_seq, grad_seq = operands
    scale = 1.0 / math.sqrt(HEAD_DIM)
    query_view = query_seq.astype(jnp.float32).reshape(SEQ, KV_HEADS, GROUP, HEAD_DIM).transpose(1, 0, 2, 3)
    grad_view = grad_seq.astype(jnp.float32).reshape(SEQ, KV_HEADS, GROUP, HEAD_DIM).transpose(1, 0, 2, 3)
    key_view = key_seq.astype(jnp.float32).reshape(SEQ, KV_HEADS, HEAD_DIM).transpose(1, 0, 2)
    value_view = value_seq.astype(jnp.float32).reshape(SEQ, KV_HEADS, HEAD_DIM).transpose(1, 0, 2)
    causal = jnp.arange(SEQ)[None, :] <= jnp.arange(SEQ)[:, None]

    def per_head(parts):
        query_part, key_part, value_part, grad_part = parts
        scores = jnp.einsum('qgd,sd->gqs', query_part, key_part) * scale
        scores = jnp.where(causal[None], scores, NEGATIVE_FILL)
        row_max = lax.optimization_barrier(jnp.max(scores, axis=-1, keepdims=True))
        log_total = row_max + jnp.log(lax.optimization_barrier(jnp.sum(jnp.exp(scores - row_max), axis=-1, keepdims=True)))
        probs = jnp.exp(scores - log_total)
        probs_low = lax.optimization_barrier(probs.astype(jnp.bfloat16)).astype(jnp.float32)
        output = jnp.einsum('gqs,sd->qgd', probs_low, value_part)
        row_delta = lax.optimization_barrier(jnp.sum(grad_part * output, axis=-1)).transpose(1, 0)[..., None]
        prob_grad = jnp.einsum('qgd,sd->gqs', grad_part, value_part)
        score_grad = probs * (prob_grad - row_delta) * scale
        score_low = lax.optimization_barrier(score_grad.astype(jnp.bfloat16)).astype(jnp.float32)
        query_grad = jnp.einsum('gqs,sd->qgd', score_low, key_part).astype(jnp.bfloat16)
        key_grad = jnp.einsum('gqs,qgd->sd', score_low, query_part).astype(jnp.bfloat16)
        value_grad = jnp.einsum('gqs,qgd->sd', probs_low, grad_part).astype(jnp.bfloat16)
        return (query_grad, key_grad, value_grad)
    query_grad, key_grad, value_grad = lax.map(per_head, (query_view, key_view, value_view, grad_view))
    query_grad = query_grad.transpose(1, 0, 2, 3).reshape(SEQ, HEADS * HEAD_DIM)
    key_grad = key_grad.transpose(1, 0, 2).reshape(SEQ, KV_HEADS * HEAD_DIM)
    value_grad = value_grad.transpose(1, 0, 2).reshape(SEQ, KV_HEADS * HEAD_DIM)
    return (query_grad, key_grad, value_grad)

def reference(ffn_input, gate_act, up_act, hidden_grad, stream_grad, w_gate, w_up, gate_keep, up_keep, w_out, queries, keys, values):
    tokens = SEQS * SEQ
    gate_f = gate_act.astype(jnp.float32)
    sigma = jax.nn.sigmoid(gate_f)
    hidden_f = hidden_grad.astype(jnp.float32)
    up_grad = (hidden_f * gate_f * sigma).astype(jnp.bfloat16).reshape(tokens, FF)
    gate_grad = (hidden_f * up_act.astype(jnp.float32) * sigma * (1.0 + gate_f * (1.0 - sigma))).astype(jnp.bfloat16).reshape(tokens, FF)
    gate_mask = widened(gate_keep)
    up_mask = widened(up_keep)
    gate_eff = w_gate * gate_mask.astype(jnp.bfloat16)
    up_eff = w_up * up_mask.astype(jnp.bfloat16)
    input_grad = jnp.dot(gate_grad, gate_eff.T, preferred_element_type=jnp.float32) + jnp.dot(up_grad, up_eff.T, preferred_element_type=jnp.float32)
    stream_total = (stream_grad.reshape(tokens, D).astype(jnp.float32) + input_grad).astype(jnp.bfloat16)
    head_grad = jnp.dot(stream_total, w_out.T, preferred_element_type=jnp.float32).astype(jnp.bfloat16)
    input_rows = ffn_input.reshape(tokens, D)
    grad_w_gate = (jnp.dot(input_rows.T, gate_grad, preferred_element_type=jnp.float32) * gate_mask).astype(jnp.bfloat16)
    grad_w_up = (jnp.dot(input_rows.T, up_grad, preferred_element_type=jnp.float32) * up_mask).astype(jnp.bfloat16)
    query_grad, key_grad, value_grad = lax.map(attention_backward, (queries, keys, values, head_grad.reshape(SEQS, SEQ, HEADS * HEAD_DIM)))
    return (grad_w_gate, grad_w_up, query_grad, key_grad, value_grad)
```

```python
import math

import jax
import jax.numpy as jnp
from jax import lax
from jax.experimental import pallas as pl
from jax.experimental.pallas import tpu as pltpu
from jax.sharding import PartitionSpec as P

MESH = pl.DeviceIdType.MESH
F32 = jnp.float32
BF16 = jnp.bfloat16

ROWS = 80
HID = 1792
WIDE = HID + 128
HALF = 1024
FEAT = 256
SEQ = 1280
HEADS = 8
HD = 128
QS = HEADS * ROWS
SCALE = 1.0 / math.sqrt(HD)
NEGATIVE_FILL = -1e30
N_COPIES = 160
OFFSETS = (-1, 1, 2)


def early_chunk(i):
    return i // 3 - 1, i % 3 - 1


def late_chunk(i):
    s, last = i // 4, i // 7
    a = (1 - s) * 3 + s * (i - 4) - last
    b = (1 - s) * i + s * 3 - last
    return a - 1, b - 1


CHUNKS = (early_chunk, late_chunk)


def nt(left, right):
    return lax.dot_general(left, right, (((1,), (1,)), ((), ())), preferred_element_type=F32)


def nn(left, right):
    return lax.dot_general(left, right, (((1,), (0,)), ((), ())), preferred_element_type=F32)


def kernel(
    ffn_hbm,
    gate_ref,
    up_ref,
    hidden_ref,
    stream_hbm,
    wg_hbm,
    wu_hbm,
    gk_ref,
    uk_ref,
    wo_hbm,
    q_hbm,
    k_ref,
    v_ref,
    gw_hbm,
    uw_hbm,
    dq_ref,
    dk_ref,
    dv_ref,
    ga,
    ua,
    w_eff,
    ffn_v,
    ffn_t,
    wout_v,
    q_v,
    q_s,
    stream_v,
    acc,
    zs,
    zr,
    strm,
    hp,
    ra,
    rb,
    ha,
    hb,
    ra2,
    rb2,
    g_own,
    g_s,
    w_send,
    w_recv,
    w_out_v,
    k_t,
    p_f,
    p_low,
    ds_s,
    kt_s,
    vt_s,
    kt_r,
    vt_r,
    kt2_s,
    vt2_s,
    kt2_r,
    vt2_r,
    send_sem,
    recv_sem,
    local_sem,
):
    row = lax.axis_index("row")
    z = lax.axis_index("col")
    core = lax.axis_index("dp")
    y, x = row // 4, row % 4

    def ring(v, off):
        return lax.rem(v + (off + 4), 4)

    def dev(axis, off):
        if axis == "x":
            return {"row": y * 4 + ring(x, off)}
        return {"row": ring(y, off) * 4 + x}

    copies = []

    def send(src, dst, device):
        i = len(copies)
        copy = pltpu.make_async_remote_copy(
            src_ref=src,
            dst_ref=dst,
            send_sem=send_sem.at[i],
            recv_sem=recv_sem.at[i],
            device_id=device,
            device_id_type=MESH,
        )
        copy.start()
        copies.append(copy)
        return copy

    barrier = pltpu.get_barrier_semaphore()
    partners = [dev("x", o) for o in OFFSETS] + [dev("y", o) for o in OFFSETS]
    partners += [{"col": lax.rem(z + o, 8)} for o in range(1, 8)] + [{"dp": 1 - core}]
    for partner in partners:
        pl.semaphore_signal(barrier, inc=1, device_id=partner, device_id_type=MESH)

    def fetch(i, src, dst):
        copy = pltpu.make_async_copy(src, dst, local_sem.at[i])
        copy.start()
        return copy

    def place(chunk):
        dy, dx = chunk
        return lax.rem(y + dy + 4, 4), lax.rem(x + dx + 4, 4)

    mine = [place(CHUNKS[b](z)) for b in range(2)]
    get_wg = fetch(0, wg_hbm, w_eff.at[0])
    get_wu = fetch(1, wu_hbm, w_eff.at[1])
    get_ffn = fetch(2, ffn_hbm.at[0], ffn_v)
    get_wo = fetch(3, wo_hbm, wout_v)
    get_q = fetch(4, q_hbm.at[0], q_v)
    get_st = [
        fetch(5 + b, stream_hbm.at[mine[b][0] * 4 + mine[b][1]], stream_v.at[b]) for b in range(2)
    ]

    def act_step(i, _):
        cols = pl.ds(pl.multiple_of(i * 128, 128), 128)
        gate_f = gate_ref[0, :, cols].astype(F32)
        hidden_f = hidden_ref[0, :, cols].astype(F32)
        sigma = jax.nn.sigmoid(gate_f)
        ua[y, x, :, cols] = (hidden_f * gate_f * sigma).astype(BF16)
        ga[y, x, :, cols] = (
            hidden_f * up_ref[0, :, cols].astype(F32) * sigma * (1.0 + gate_f * (1.0 - sigma))
        ).astype(BF16)
        return 0

    lax.fori_loop(0, HID // 128, act_step, 0)
    ga[y, x, :, HID:] = k_ref[0]
    ua[y, x, :, HID:] = v_ref[0]

    pl.semaphore_wait(barrier, len(partners))

    arrays = ((ga, "x", "y"), (ua, "y", "x"))

    def at(n, first, second):
        arr, p, _ = arrays[n]
        if p == "x":
            return arr.at[ring(y, second), ring(x, first)]
        return arr.at[ring(y, first), ring(x, second)]

    along, relay, across, far = {}, {}, {}, {}

    def spread(n, first):
        block = at(n, first, 0)
        for d in (1, -1):
            across[n, first, d] = send(block, block, dev(arrays[n][2], d))

    for n in range(2):
        for d in (1, -1):
            along[n, d] = send(at(n, 0, 0), at(n, 0, 0), dev(arrays[n][1], d))
    for n in range(2):
        spread(n, 0)

    for n, (get, keep) in enumerate(((get_wg, gk_ref), (get_wu, uk_ref))):
        get.wait()

        def mask_step(j, _, n=n, keep=keep):
            cols = pl.ds(pl.multiple_of(j * 128, 128), 128)
            for i in range(2):
                rows = slice(i * 128, (i + 1) * 128)
                tile = w_eff[n, rows, cols].astype(F32) * keep[i, j].astype(F32)
                w_eff[n, rows, cols] = tile.astype(BF16)
            return 0

        lax.fori_loop(0, HID // 128, mask_step, 0)

    for d in (1, -1):
        for n in range(2):
            along[n, d].wait_recv()
            cols = slice(0, HALF) if d == 1 else slice(HALF, WIDE)
            part = at(n, -d, 0).at[:, cols]
            relay[n, d] = send(part, part, dev(arrays[n][1], d))
            spread(n, -d)

    get_ffn.wait()

    def transpose_step(i, _):
        rows = pl.ds(pl.multiple_of(i * 256, 256), 256)
        ffn_t[:, rows] = ffn_v[rows, :].T
        return 0

    lax.fori_loop(0, SEQ // 256, transpose_step, 0)
    get_q.wait()
    for h in range(HEADS):
        q_s[h * ROWS : (h + 1) * ROWS, :] = q_v[:, h * HD : (h + 1) * HD]

    for n in range(2):
        relay[n, 1].wait_recv()
        relay[n, -1].wait_recv()
        spread(n, 2)

    for first in (0, -1, 1, 2):
        for n in range(2):
            across[n, first, 1].wait_recv()
            across[n, first, -1].wait_recv()
            d = 1 if first in (0, -1) else -1
            far[n, first] = send(at(n, first, -d), at(n, first, -d), dev(arrays[n][2], d))

    def input_terms(b):
        for half in range(2):
            spots = [place(CHUNKS[b](half * 4 + i)) for i in range(4)]

            def step(t, _):
                cols = pl.ds(pl.multiple_of(t * 256, 256), 256)
                gate_x = jnp.concatenate([ga[yc, xc, :, cols] for yc, xc in spots], axis=0)
                up_x = jnp.concatenate([ua[yc, xc, :, cols] for yc, xc in spots], axis=0)
                acc[...] += nt(gate_x, w_eff[0, :, cols]) + nt(up_x, w_eff[1, :, cols])
                return 0

            acc[...] = jnp.zeros_like(acc)
            lax.fori_loop(0, HID // 256, step, 0)
            for i in range(4):
                zs[b, half * 4 + i] = acc[i * ROWS : (i + 1) * ROWS, :].astype(BF16)

    def scatter_col(b):
        out = []
        for off in range(1, 8):
            to = lax.rem(z + off, 8)
            out.append(send(zs.at[b, to], zr.at[b, off - 1], {"col": to}))
        return out

    def gather_col(b, pending):
        for copy in pending:
            copy.wait_recv()
        get_st[b].wait()
        total = zs[b, z].astype(F32)
        for j in range(7):
            total += zr[b, j].astype(F32)
        yc, xc = mine[b]
        strm[yc, xc] = (stream_v[b].astype(F32) + total).astype(BF16)
        block = strm.at[yc, xc]
        return [send(block, block, {"col": lax.rem(z + off, 8)}) for off in range(1, 8)]

    first_a, first_b = {}, {}

    def head_terms(b, pending):
        for copy in pending:
            copy.wait_recv()
        for half in range(2):
            chunks = [CHUNKS[b](half * 4 + i) for i in range(4)]
            spots = [place(c) for c in chunks]
            total = jnp.concatenate([strm[yc, xc] for yc, xc in spots], axis=0)

            def step(t, _):
                cols = pl.ds(pl.multiple_of(t * 256, 256), 256)
                part = nt(total, wout_v[cols, :]).astype(BF16)
                for i, (yc, xc) in enumerate(spots):
                    hp[yc, xc, :, cols] = part[i * ROWS : (i + 1) * ROWS, :]
                return 0

            lax.fori_loop(0, 4, step, 0)
            for (dy, dx), (yc, xc) in zip(chunks, spots):
                if dx != 0:
                    first_a[dy, dx] = send(
                        hp.at[yc, xc, :, 0:512], ra.at[OFFSETS.index(dx), yc], dev("x", dx)
                    )
                if dy != 0:
                    first_b[dy, dx] = send(
                        hp.at[yc, xc, :, 512:1024], rb.at[OFFSETS.index(dy), xc], dev("y", dy)
                    )

    input_terms(0)
    rs0 = scatter_col(0)
    for n in range(2):
        for first in (0, -1, 1, 2):
            far[n, first].wait_recv()
    input_terms(1)
    rs1 = scatter_col(1)
    ag0 = gather_col(0, rs0)

    def wgrad(n):
        arr = arrays[n][0]

        def step(t, _):
            cols = pl.ds(pl.multiple_of(t * 256, 256), 256)
            tokens = arr[:, :, :, cols].reshape(SEQ, 256)
            w_send[n, :, cols] = nn(ffn_t[...], tokens).astype(BF16)
            return 0

        lax.fori_loop(0, HID // 256, step, 0)
        return send(w_send.at[n], w_recv.at[n], {"dp": 1 - core})

    get_wo.wait()
    ag1 = gather_col(1, rs1)
    head_terms(0, ag0)
    pair = [wgrad(0), wgrad(1)]
    head_terms(1, ag1)

    keys = ga[:, :, :, HID:].reshape(SEQ, HD)
    k_t[...] = keys.T

    def softmax_step(t, _):
        cols = pl.ds(pl.multiple_of(t * 128, 128), 128)
        scores = nt(ga[:, :, :, HID:].reshape(SEQ, HD), q_s[cols, :]) * SCALE
        lane = lax.broadcasted_iota(jnp.int32, (1, 128), 1) + t * 128
        head = jnp.zeros_like(lane)
        for h in range(1, HEADS):
            head += (lane >= h * ROWS).astype(jnp.int32)
        query_pos = lane - head * ROWS + row * ROWS
        key_pos = lax.broadcasted_iota(jnp.int32, (SEQ, 128), 0)
        scores = jnp.where(key_pos <= query_pos, scores, NEGATIVE_FILL)
        weight = jnp.exp(scores - jnp.max(scores, axis=0, keepdims=True))
        probs = weight * (1.0 / jnp.sum(weight, axis=0, keepdims=True))
        p_f[:, cols] = probs
        p_low[:, cols] = probs.astype(BF16)
        return 0

    lax.fori_loop(0, QS // 128, softmax_step, 0)

    second_a, second_b = {}, {}
    for off in (2, -1, 1, 0):
        for other in OFFSETS:
            first_a[off, other].wait_recv()
            first_b[other, off].wait_recv()
        yc, xc = ring(y, off), ring(x, off)
        total_a = hp[yc, x, :, 0:512].astype(F32)
        total_b = hp[y, xc, :, 512:1024].astype(F32)
        for k in range(3):
            total_a += ra[k, yc].astype(F32)
            total_b += rb[k, xc].astype(F32)
        if off == 0:
            g_own[:, 0:512] = total_a
            g_own[:, 512:1024] = total_b
        else:
            k = OFFSETS.index(off)
            ha[k] = total_a.astype(BF16)
            hb[k] = total_b.astype(BF16)
            second_a[k] = send(ha.at[k], ra2.at[k], dev("y", off))
            second_b[k] = send(hb.at[k], rb2.at[k], dev("x", off))

    put = []
    for n, (keep, out) in enumerate(((gk_ref, gw_hbm), (uk_ref, uw_hbm))):
        pair[n].wait_recv()

        def sum_step(j, _, n=n, keep=keep):
            cols = pl.ds(pl.multiple_of(j * 128, 128), 128)
            for i in range(2):
                rows = slice(i * 128, (i + 1) * 128)
                total = w_send[n, rows, cols].astype(F32) + w_recv[n, rows, cols].astype(F32)
                w_out_v[n, rows, cols] = (total * keep[i, j].astype(F32)).astype(BF16)
            return 0

        lax.fori_loop(0, HID // 128, sum_step, 0)
        put.append(fetch(7 + n, w_out_v.at[n], out))

    for k in range(3):
        second_a[k].wait_recv()
        second_b[k].wait_recv()
    for h in range(HEADS):
        cols = slice(h * HD, (h + 1) * HD)
        total = g_own[:, cols]
        buf = ra2 if h < 4 else rb2
        low = slice((h % 4) * HD, (h % 4 + 1) * HD)
        for k in range(3):
            total += buf[k, :, low].astype(F32)
        g_s[h * ROWS : (h + 1) * ROWS, :] = total.astype(BF16)

    def v_step(t, _):
        rows = pl.ds(pl.multiple_of(t * 320, 320), 320)
        part = nn(p_low[rows, :], g_s[...]).astype(BF16)
        for i in range(4):
            vt_s[t, i] = part[i * ROWS : (i + 1) * ROWS, :]
        return 0

    lax.fori_loop(0, 4, v_step, 0)
    val1 = [send(vt_s.at[ring(y, o)], vt_r.at[k], dev("y", o)) for k, o in enumerate(OFFSETS)]

    def score_step(t, _):
        cols = pl.ds(pl.multiple_of(t * 128, 128), 128)
        prob_grad = nt(ua[:, :, :, HID:].reshape(SEQ, HD), g_s[cols, :])
        delta = jnp.sum(p_low[:, cols].astype(F32) * prob_grad, axis=0, keepdims=True)
        ds_s[:, cols] = (p_f[:, cols] * (prob_grad - delta) * SCALE).astype(BF16)
        return 0

    lax.fori_loop(0, QS // 128, score_step, 0)

    def k_step(t, _):
        rows = pl.ds(pl.multiple_of(t * 320, 320), 320)
        part = nn(ds_s[rows, :], q_s[...]).astype(BF16)
        for i in range(4):
            kt_s[i, t] = part[i * ROWS : (i + 1) * ROWS, :]
        return 0

    lax.fori_loop(0, 4, k_step, 0)
    key1 = [send(kt_s.at[ring(x, o)], kt_r.at[k], dev("x", o)) for k, o in enumerate(OFFSETS)]

    def q_step(t, _):
        cols = pl.ds(pl.multiple_of(t * 128, 128), 128)
        q_s[cols, :] = nn(k_t[...], ds_s[:, cols]).T.astype(BF16)
        return 0

    lax.fori_loop(0, QS // 128, q_step, 0)
    for h in range(HEADS):
        dq_ref[0, :, h * HD : (h + 1) * HD] = q_s[h * ROWS : (h + 1) * ROWS, :]

    def reduce(first, own_group, recv, buf, axis, keep_at, landing):
        for copy in first:
            copy.wait_recv()
        out = []
        for k, o in enumerate(OFFSETS):
            spot = ring(keep_at, o)
            total = own_group[spot].astype(F32)
            for j in range(3):
                total += recv[j, spot].astype(F32)
            buf[k] = total.astype(BF16)
            out.append(send(buf.at[k], landing.at[k], dev(axis, o)))
        total = own_group[keep_at].astype(F32)
        for j in range(3):
            total += recv[j, keep_at].astype(F32)
        return total, out

    val_own, val2 = reduce(val1, vt_s.at[y], vt_r, vt2_s, "x", x, vt2_r)
    key_own, key2 = reduce(key1, kt_s.at[x], kt_r, kt2_s, "y", y, kt2_r)
    for own, second, landing, out in (
        (val_own, val2, vt2_r, dv_ref),
        (key_own, key2, kt2_r, dk_ref),
    ):
        for copy in second:
            copy.wait_recv()
        for k in range(3):
            own += landing[k].astype(F32)
        out[0] = own.astype(BF16)

    for copy in copies:
        copy.wait_send()
    for copy in put:
        copy.wait()


def on_device(
    ffn_input,
    gate_act,
    up_act,
    hidden_grad,
    stream_grad,
    w_gate,
    w_up,
    gate_keep,
    up_keep,
    w_out,
    queries,
    keys,
    values,
):
    hbm = pl.BlockSpec(memory_space=pl.ANY)
    vmem = pl.BlockSpec(memory_space=pltpu.VMEM)
    smem = pl.BlockSpec(memory_space=pltpu.SMEM)
    chunk_grid = (4, 4, ROWS)
    return pl.pallas_call(
        kernel,
        out_shape=(
            jax.ShapeDtypeStruct((FEAT, HID), BF16),
            jax.ShapeDtypeStruct((FEAT, HID), BF16),
            jax.ShapeDtypeStruct((1, ROWS, HEADS * HD), BF16),
            jax.ShapeDtypeStruct((1, ROWS, HD), BF16),
            jax.ShapeDtypeStruct((1, ROWS, HD), BF16),
        ),
        in_specs=[hbm, vmem, vmem, vmem, hbm, hbm, hbm, smem, smem, hbm, hbm, vmem, vmem],
        out_specs=(hbm, hbm, vmem, vmem, vmem),
        scratch_shapes=[
            pltpu.VMEM(chunk_grid + (WIDE,), BF16),
            pltpu.VMEM(chunk_grid + (WIDE,), BF16),
            pltpu.VMEM((2, FEAT, HID), BF16),
            pltpu.VMEM((SEQ, FEAT), BF16),
            pltpu.VMEM((FEAT, SEQ), BF16),
            pltpu.VMEM((HEADS * HD, FEAT), BF16),
            pltpu.VMEM((ROWS, HEADS * HD), BF16),
            pltpu.VMEM((QS, HD), BF16),
            pltpu.VMEM((2, ROWS, FEAT), BF16),
            pltpu.VMEM((4 * ROWS, FEAT), F32),
            pltpu.VMEM((2, 8, ROWS, FEAT), BF16),
            pltpu.VMEM((2, 7, ROWS, FEAT), BF16),
            pltpu.VMEM(chunk_grid + (FEAT,), BF16),
            pltpu.VMEM(chunk_grid + (HEADS * HD,), BF16),
            pltpu.VMEM((3, 4, ROWS, 512), BF16),
            pltpu.VMEM((3, 4, ROWS, 512), BF16),
            pltpu.VMEM((3, ROWS, 512), BF16),
            pltpu.VMEM((3, ROWS, 512), BF16),
            pltpu.VMEM((3, ROWS, 512), BF16),
            pltpu.VMEM((3, ROWS, 512), BF16),
            pltpu.VMEM((ROWS, HEADS * HD), F32),
            pltpu.VMEM((QS, HD), BF16),
            pltpu.VMEM((2, FEAT, HID), BF16),
            pltpu.VMEM((2, FEAT, HID), BF16),
            pltpu.VMEM((2, FEAT, HID), BF16),
            pltpu.VMEM((HD, SEQ), BF16),
            pltpu.VMEM((SEQ, QS), F32),
            pltpu.VMEM((SEQ, QS), BF16),
            pltpu.VMEM((SEQ, QS), BF16),
            pltpu.VMEM(chunk_grid + (HD,), BF16),
            pltpu.VMEM(chunk_grid + (HD,), BF16),
            pltpu.VMEM((3, 4, ROWS, HD), BF16),
            pltpu.VMEM((3, 4, ROWS, HD), BF16),
            pltpu.VMEM((3, ROWS, HD), BF16),
            pltpu.VMEM((3, ROWS, HD), BF16),
            pltpu.VMEM((3, ROWS, HD), BF16),
            pltpu.VMEM((3, ROWS, HD), BF16),
            pltpu.SemaphoreType.DMA((N_COPIES,)),
            pltpu.SemaphoreType.DMA((N_COPIES,)),
            pltpu.SemaphoreType.DMA((9,)),
        ],
        compiler_params=pltpu.CompilerParams(
            collective_id=0, has_side_effects=True, vmem_limit_bytes=56 * 1024 * 1024
        ),
    )(
        ffn_input,
        gate_act,
        up_act,
        hidden_grad,
        stream_grad.reshape(16, ROWS, FEAT),
        w_gate,
        w_up,
        gate_keep,
        up_keep,
        w_out,
        queries,
        keys,
        values,
    )


def solution(mesh):
    placed = (
        P("dp", None, "row"),
        P("dp", "row", "col"),
        P("dp", "row", "col"),
        P("dp", "row", "col"),
        P("dp", None, "row"),
        P("row", "col"),
        P("row", "col"),
        P("row", "col"),
        P("row", "col"),
        P("col", "row"),
        P("dp", "row", "col"),
        P("dp", "row", "col"),
        P("dp", "row", "col"),
    )
    return jax.shard_map(
        on_device,
        mesh=mesh,
        in_specs=placed,
        out_specs=(
            P("row", "col"),
            P("row", "col"),
            P("dp", "row", "col"),
            P("dp", "row", "col"),
            P("dp", "row", "col"),
        ),
        check_vma=False,
    )
```

```python
import math

import jax
import jax.numpy as jnp
from jax import lax
from jax.experimental import pallas as pl
from jax.experimental.pallas import tpu as pltpu
from jax.sharding import PartitionSpec as P

MESH = pl.DeviceIdType.MESH
F32 = jnp.float32
BF16 = jnp.bfloat16

ROWS = 80
CUT = 48
PARTS = 4
HID = 1792
WIDE = HID + 128
HALF = 1024
FEAT = 256
SEQ = 1280
HEADS = 8
HD = 128
QS = HEADS * ROWS
SCALE = 1.0 / math.sqrt(HD)
NEGATIVE_FILL = -1e30
N_GROUPS = 46
OFFSETS = (-1, 1, 2)

QUARTERS = (
    ((0, 0), (0, -1), (-1, 0), (-1, -1)),
    ((0, 1), (1, 0), (-1, 1), (1, -1)),
    ((0, 2), (2, 0), (1, 2), (2, 1)),
    ((1, 1), (-1, 2), (2, -1), (2, 2)),
)


def pick(table, j):
    total = 0
    for k, value in enumerate(table):
        total = total + value * (1 - lax.div(lax.rem(j + (4 - k), 4) + 3, 4))
    return total


def nt(left, right):
    return lax.dot_general(left, right, (((1,), (1,)), ((), ())), preferred_element_type=F32)


def nn(left, right):
    return lax.dot_general(left, right, (((1,), (0,)), ((), ())), preferred_element_type=F32)


def kernel(
    ffn_hbm,
    gate_ref,
    up_ref,
    hidden_ref,
    stream_hbm,
    wg_hbm,
    wu_hbm,
    gk_ref,
    uk_ref,
    wo_hbm,
    q_hbm,
    k_ref,
    v_ref,
    gw_hbm,
    uw_hbm,
    dq_ref,
    dk_ref,
    dv_ref,
    ga,
    ua,
    w_eff,
    ffn_v,
    ffn_t,
    wout_v,
    q_v,
    q_s,
    stream_v,
    zs,
    zr,
    strm,
    hp,
    ra,
    rb,
    ha,
    hb,
    ra2,
    rb2,
    g_own,
    g_s,
    w_send,
    w_recv,
    w_out_v,
    k_t,
    p_f,
    p_low,
    ds_s,
    kt_s,
    vt_s,
    kta_r,
    ktb_r,
    vt_r,
    kta2_s,
    ktb2_s,
    vt2_s,
    kta2_r,
    ktb2_r,
    vt2_r,
    send_sem,
    recv_sem,
    local_sem,
):
    row = lax.axis_index("row")
    z = lax.axis_index("col")
    core = lax.axis_index("dp")
    y, x = row // 4, row % 4

    def ring(v, off):
        return lax.rem(v + (off + 4), 4)

    def dev(axis, off):
        if axis == "x":
            return {"row": y * 4 + ring(x, off)}
        return {"row": ring(y, off) * 4 + x}

    groups = []

    class Group:
        def __init__(self, size):
            self.i, self.size = len(groups), size
            groups.append(self)

        def copy(self, src, dst, device):
            return pltpu.make_async_remote_copy(
                src_ref=src,
                dst_ref=dst,
                send_sem=send_sem.at[self.i],
                recv_sem=recv_sem.at[self.i],
                device_id=device,
                device_id_type=MESH,
            )

        def send(self, src, dst, device):
            self.copy(src, dst, device).start()

        def wait_recv(self):
            self.copy(self.size, self.size, {"dp": 1 - core}).wait_recv()

        def wait_send(self):
            self.copy(self.size, self.size, {"dp": 1 - core}).wait_send()

    barrier = pltpu.get_barrier_semaphore()
    partners = [dev("x", o) for o in OFFSETS] + [dev("y", o) for o in OFFSETS]
    partners += [{"col": lax.rem(z + o, 8)} for o in range(1, 8)] + [{"dp": 1 - core}]
    for partner in partners:
        pl.semaphore_signal(barrier, inc=1, device_id=partner, device_id_type=MESH)

    def fetch(i, src, dst):
        copy = pltpu.make_async_copy(src, dst, local_sem.at[i])
        copy.start()
        return copy

    def place(chunk):
        dy, dx = chunk
        return lax.rem(y + dy + 4, 4), lax.rem(x + dx + 4, 4)

    mine = []
    for quarter in QUARTERS:
        mine.append(place([pick([chunk[i] for chunk in quarter], z // 2) for i in range(2)]))
    side = lax.rem(z, 2)
    side_cols = pl.ds(pl.multiple_of(side * HD, HD), HD)
    get_wg = fetch(0, wg_hbm, w_eff.at[0])
    get_wu = fetch(1, wu_hbm, w_eff.at[1])
    get_ffn = fetch(2, ffn_hbm.at[0], ffn_v)
    get_wo = fetch(3, wo_hbm, wout_v)
    get_q = fetch(4, q_hbm.at[0], q_v)
    get_st = [
        fetch(5 + b, stream_hbm.at[mine[b][0] * 4 + mine[b][1], :, side_cols], stream_v.at[b])
        for b in range(4)
    ]

    def act_step(i, _):
        cols = pl.ds(pl.multiple_of(i * 128, 128), 128)
        gate_f = gate_ref[0, :, cols].astype(F32)
        hidden_f = hidden_ref[0, :, cols].astype(F32)
        sigma = jax.nn.sigmoid(gate_f)
        ua[y, x, :, cols] = (hidden_f * gate_f * sigma).astype(BF16)
        ga[y, x, :, cols] = (
            hidden_f * up_ref[0, :, cols].astype(F32) * sigma * (1.0 + gate_f * (1.0 - sigma))
        ).astype(BF16)
        return 0

    lax.fori_loop(0, HID // 128, act_step, 0)
    ga[y, x, :, HID:] = k_ref[0]
    ua[y, x, :, HID:] = v_ref[0]

    pl.semaphore_wait(barrier, len(partners))

    arrays = ((ga, "x", "y"), (ua, "y", "x"))

    def at(n, first, second):
        arr, p, _ = arrays[n]
        if p == "x":
            return arr.at[ring(y, second), ring(x, first)]
        return arr.at[ring(y, first), ring(x, second)]

    two_chunks = ga.at[0, 0:2]
    along = {(n, d): Group(at(n, 0, 0)) for n in range(2) for d in (1, -1)}
    relay = [Group(at(n, 2, 0)) for n in range(2)]
    across = {(n, first): Group(two_chunks) for n in range(2) for first in (0, -1, 1, 2)}
    far = {(n, part): Group(two_chunks) for n in range(2) for part in range(2)}

    def spread(n, first):
        block = at(n, first, 0)
        for d in (1, -1):
            across[n, first].send(block, block, dev(arrays[n][2], d))

    for n in range(2):
        for d in (1, -1):
            along[n, d].send(at(n, 0, 0), at(n, 0, 0), dev(arrays[n][1], d))
    for n in range(2):
        spread(n, 0)

    for n, (get, keep) in enumerate(((get_wg, gk_ref), (get_wu, uk_ref))):
        get.wait()

        def mask_step(j, _, n=n, keep=keep):
            cols = pl.ds(pl.multiple_of(j * 128, 128), 128)
            for i in range(2):
                rows = slice(i * 128, (i + 1) * 128)
                tile = w_eff[n, rows, cols].astype(F32) * keep[i, j].astype(F32)
                w_eff[n, rows, cols] = tile.astype(BF16)
            return 0

        lax.fori_loop(0, HID // 128, mask_step, 0)

    for d in (1, -1):
        for n in range(2):
            along[n, d].wait_recv()
            cols = slice(0, HALF) if d == 1 else slice(HALF, WIDE)
            part = at(n, -d, 0).at[:, cols]
            relay[n].send(part, part, dev(arrays[n][1], d))
            spread(n, -d)

    get_ffn.wait()

    def transpose_step(i, _):
        rows = pl.ds(pl.multiple_of(i * 256, 256), 256)
        ffn_t[:, rows] = ffn_v[rows, :].T
        return 0

    lax.fori_loop(0, SEQ // 256, transpose_step, 0)
    get_q.wait()
    for h in range(HEADS):
        q_s[h * ROWS : (h + 1) * ROWS, :] = q_v[:, h * HD : (h + 1) * HD]

    for n in range(2):
        relay[n].wait_recv()
        spread(n, 2)

    for first, d, part in ((0, 1, 0), (-1, 1, 1), (1, -1, 0), (2, -1, 1)):
        for n in range(2):
            across[n, first].wait_recv()
            block = at(n, first, -d)
            far[n, part].send(block, block, dev(arrays[n][2], d))

    col_sum = [Group(zr.at[b]) for b in range(4)]
    col_all = [Group(zr.at[b]) for b in range(4)]

    def input_terms(b):
        spots = [place(c) for c in QUARTERS[b]]
        gate_x = jnp.concatenate([ga[yc, xc, :, 0:HID] for yc, xc in spots], axis=0)
        total = nt(gate_x, w_eff[0])
        up_x = jnp.concatenate([ua[yc, xc, :, 0:HID] for yc, xc in spots], axis=0)
        total += nt(up_x, w_eff[1])
        for i in range(4):
            for j in range(2):
                zs[b, i * 2 + j] = total[
                    i * ROWS : (i + 1) * ROWS, j * HD : (j + 1) * HD
                ].astype(BF16)
        for off in range(1, 8):
            to = lax.rem(z + off, 8)
            col_sum[b].send(zs.at[b, to], zr.at[b, off - 1], {"col": to})

    def gather_col(b):
        col_sum[b].wait_recv()
        get_st[b].wait()
        total = zs[b, z].astype(F32)
        for j in range(7):
            total += zr[b, j].astype(F32)
        yc, xc = mine[b]
        strm[yc, xc, side] = (stream_v[b].astype(F32) + total).astype(BF16)
        block = strm.at[yc, xc, side]
        for off in range(1, 8):
            col_all[b].send(block, block, {"col": lax.rem(z + off, 8)})

    first_a = {dy: Group(ra2) for dy in (0, -1, 1, 2)}
    first_b = {dx: Group(rb2) for dx in (0, -1, 1, 2)}

    def head_terms(b):
        col_all[b].wait_recv()
        spots = [place(c) for c in QUARTERS[b]]
        total = jnp.concatenate(
            [
                jnp.concatenate([strm[yc, xc, j] for yc, xc in spots], axis=0) for j in range(2)
            ],
            axis=1,
        )

        def step(t, _):
            cols = pl.ds(pl.multiple_of(t * 256, 256), 256)
            part = nt(total, wout_v[cols, :]).astype(BF16)
            for i, (yc, xc) in enumerate(spots):
                hp[yc, xc, :, cols] = part[i * ROWS : (i + 1) * ROWS, :]
            return 0

        lax.fori_loop(0, 4, step, 0)
        for (dy, dx), (yc, xc) in zip(QUARTERS[b], spots):
            if dx != 0:
                first_a[dy].send(
                    hp.at[yc, xc, :, 0:512], ra.at[OFFSETS.index(dx), yc], dev("x", dx)
                )
            if dy != 0:
                first_b[dx].send(
                    hp.at[yc, xc, :, 512:1024], rb.at[OFFSETS.index(dy), xc], dev("y", dy)
                )

    input_terms(0)
    input_terms(1)
    gather_col(0)
    gather_col(1)
    for part in range(2):
        for n in range(2):
            far[n, part].wait_recv()
        input_terms(2 + part)

    def wgrad(n):
        arr = arrays[n][0]

        def step(t, _):
            cols = pl.ds(pl.multiple_of(t * 256, 256), 256)
            tokens = arr[:, :, :, cols].reshape(SEQ, 256)
            w_send[n, :, cols] = nn(ffn_t[...], tokens).astype(BF16)
            return 0

        lax.fori_loop(0, HID // 256, step, 0)
        pair[n].send(w_send.at[n], w_recv.at[n], {"dp": 1 - core})

    pair = [Group(w_recv.at[n]) for n in range(2)]
    gather_col(2)
    get_wo.wait()
    head_terms(0)
    head_terms(1)
    wgrad(0)
    gather_col(3)
    head_terms(2)
    wgrad(1)
    head_terms(3)

    keys = ga[:, :, :, HID:].reshape(SEQ, HD)
    k_t[...] = keys.T

    def softmax_step(t, _):
        cols = pl.ds(pl.multiple_of(t * 128, 128), 128)
        scores = nt(ga[:, :, :, HID:].reshape(SEQ, HD), q_s[cols, :]) * SCALE
        lane = lax.broadcasted_iota(jnp.int32, (1, 128), 1) + t * 128
        head = jnp.zeros_like(lane)
        for h in range(1, HEADS):
            head += (lane >= h * ROWS).astype(jnp.int32)
        query_pos = lane - head * ROWS + row * ROWS
        key_pos = lax.broadcasted_iota(jnp.int32, (SEQ, 128), 0)
        scores = jnp.where(key_pos <= query_pos, scores, NEGATIVE_FILL)
        weight = jnp.exp(scores - jnp.max(scores, axis=0, keepdims=True))
        probs = weight * (1.0 / jnp.sum(weight, axis=0, keepdims=True))
        p_f[:, cols] = probs
        p_low[:, cols] = probs.astype(BF16)
        return 0

    lax.fori_loop(0, QS // 128, softmax_step, 0)

    second_a, second_b = Group(ra2), Group(rb2)
    for off in (2, -1, 1, 0):
        first_a[off].wait_recv()
        first_b[off].wait_recv()
        yc, xc = ring(y, off), ring(x, off)
        total_a = hp[yc, x, :, 0:512].astype(F32)
        total_b = hp[y, xc, :, 512:1024].astype(F32)
        for k in range(3):
            total_a += ra[k, yc].astype(F32)
            total_b += rb[k, xc].astype(F32)
        if off == 0:
            g_own[:, 0:512] = total_a
            g_own[:, 512:1024] = total_b
        else:
            k = OFFSETS.index(off)
            ha[k] = total_a.astype(BF16)
            hb[k] = total_b.astype(BF16)
            second_a.send(ha.at[k], ra2.at[k], dev("y", off))
            second_b.send(hb.at[k], rb2.at[k], dev("x", off))

    put = []
    for n, (keep, out) in enumerate(((gk_ref, gw_hbm), (uk_ref, uw_hbm))):
        pair[n].wait_recv()

        def sum_step(j, _, n=n, keep=keep):
            cols = pl.ds(pl.multiple_of(j * 128, 128), 128)
            for i in range(2):
                rows = slice(i * 128, (i + 1) * 128)
                total = w_send[n, rows, cols].astype(F32) + w_recv[n, rows, cols].astype(F32)
                w_out_v[n, rows, cols] = (total * keep[i, j].astype(F32)).astype(BF16)
            return 0

        lax.fori_loop(0, HID // 128, sum_step, 0)
        put.append(fetch(9 + n, w_out_v.at[n], out))

    second_a.wait_recv()
    second_b.wait_recv()
    for h in range(HEADS):
        cols = slice(h * HD, (h + 1) * HD)
        total = g_own[:, cols]
        buf = ra2 if h < 4 else rb2
        low = slice((h % 4) * HD, (h % 4 + 1) * HD)
        for k in range(3):
            total += buf[k, :, low].astype(F32)
        g_s[h * ROWS : (h + 1) * ROWS, :] = total.astype(BF16)

    def v_step(t, _):
        rows = pl.ds(pl.multiple_of(t * 320, 320), 320)
        part = nn(p_low[rows, :], g_s[...]).astype(BF16)
        for i in range(4):
            vt_s[t, i] = part[i * ROWS : (i + 1) * ROWS, :]
        return 0

    lax.fori_loop(0, 4, v_step, 0, unroll=True)
    val1, val2 = Group(vt_r), Group(vt2_r)
    for k, o in enumerate(OFFSETS):
        val1.send(vt_s.at[ring(y, o)], vt_r.at[k], dev("y", o))

    def score_step(t, _):
        cols = pl.ds(pl.multiple_of(t * 128, 128), 128)
        prob_grad = nt(ua[:, :, :, HID:].reshape(SEQ, HD), g_s[cols, :])
        delta = jnp.sum(p_low[:, cols].astype(F32) * prob_grad, axis=0, keepdims=True)
        ds_s[:, cols] = (p_f[:, cols] * (prob_grad - delta) * SCALE).astype(BF16)
        return 0

    lax.fori_loop(0, QS // 128, score_step, 0, unroll=True)

    def k_step(t, _):
        rows = pl.ds(pl.multiple_of(t * 320, 320), 320)
        part = nn(ds_s[rows, :], q_s[...]).astype(BF16)
        for i in range(4):
            kt_s[t, i] = part[i * ROWS : (i + 1) * ROWS, :]
        return 0

    lax.fori_loop(0, 4, k_step, 0, unroll=True)
    keya1, keyb1 = Group(kta_r), Group(ktb_r)
    keya2, keyb2 = Group(kta2_r), Group(ktb2_r)
    for k, o in enumerate(OFFSETS):
        keya1.send(kt_s.at[:, ring(x, o), 0:CUT], kta_r.at[k], dev("x", o))
        keyb1.send(kt_s.at[ring(y, o), :, CUT:ROWS], ktb_r.at[k], dev("y", o))

    def q_step(t, _):
        cols = pl.ds(pl.multiple_of(t * 128, 128), 128)
        q_s[cols, :] = nn(k_t[...], ds_s[:, cols]).T.astype(BF16)
        return 0

    lax.fori_loop(0, QS // 128, q_step, 0)
    for h in range(HEADS):
        dq_ref[0, :, h * HD : (h + 1) * HD] = q_s[h * ROWS : (h + 1) * ROWS, :]

    def add_up(first, own, recv, buf, axis, keep_at, second, landing):
        first.wait_recv()
        for k, o in enumerate(OFFSETS):
            spot = ring(keep_at, o)
            total = own(spot).astype(F32)
            for j in range(3):
                total += recv[j, spot].astype(F32)
            buf[k] = total.astype(BF16)
            second.send(buf.at[k], landing.at[k], dev(axis, o))
        total = own(keep_at).astype(F32)
        for j in range(3):
            total += recv[j, keep_at].astype(F32)
        return total

    val_own = add_up(val1, lambda i: vt_s[y, i], vt_r, vt2_s, "x", x, val2, vt2_r)
    keya_own = add_up(
        keya1, lambda i: kt_s[i, x, 0:CUT], kta_r, kta2_s, "y", y, keya2, kta2_r
    )
    keyb_own = add_up(
        keyb1, lambda i: kt_s[y, i, CUT:ROWS], ktb_r, ktb2_s, "x", x, keyb2, ktb2_r
    )
    for own, second, landing, out, rows in (
        (val_own, val2, vt2_r, dv_ref, slice(0, ROWS)),
        (keya_own, keya2, kta2_r, dk_ref, slice(0, CUT)),
        (keyb_own, keyb2, ktb2_r, dk_ref, slice(CUT, ROWS)),
    ):
        second.wait_recv()
        for k in range(3):
            own += landing[k].astype(F32)
        out[0, rows] = own.astype(BF16)

    for group in groups:
        group.wait_send()
    for copy in put:
        copy.wait()


def hand_on(*refs):
    sources, targets, through, (get_sem, put_sem) = refs[:5], refs[5:10], refs[10:15], refs[15:]
    parts = []
    for n in range(5):
        for i in range(PARTS if n < 2 else 1):
            rows = pl.ds(i * (FEAT // PARTS), FEAT // PARTS) if n < 2 else 0
            parts.append([ref.at[rows] for ref in (sources[n], through[n], targets[n])])
    gets = [
        pltpu.make_async_copy(part[0], part[1], get_sem.at[i]) for i, part in enumerate(parts)
    ]
    puts = [
        pltpu.make_async_copy(part[1], part[2], put_sem.at[i]) for i, part in enumerate(parts)
    ]
    for get in gets:
        get.start()
    for get, put in zip(gets, puts):
        get.wait()
        put.start()
    for put in puts:
        put.wait()


def on_device(
    ffn_input,
    gate_act,
    up_act,
    hidden_grad,
    stream_grad,
    w_gate,
    w_up,
    gate_keep,
    up_keep,
    w_out,
    queries,
    keys,
    values,
):
    hbm = pl.BlockSpec(memory_space=pl.ANY)
    vmem = pl.BlockSpec(memory_space=pltpu.VMEM)
    smem = pl.BlockSpec(memory_space=pltpu.SMEM)
    chunk_grid = (4, 4, ROWS)
    out_shape = (
        jax.ShapeDtypeStruct((FEAT, HID), BF16),
        jax.ShapeDtypeStruct((FEAT, HID), BF16),
        jax.ShapeDtypeStruct((1, ROWS, HEADS * HD), BF16),
        jax.ShapeDtypeStruct((1, ROWS, HD), BF16),
        jax.ShapeDtypeStruct((1, ROWS, HD), BF16),
    )
    results = pl.pallas_call(
        kernel,
        out_shape=out_shape,
        in_specs=[hbm, vmem, vmem, vmem, hbm, hbm, hbm, smem, smem, hbm, hbm, vmem, vmem],
        out_specs=(hbm, hbm, vmem, vmem, vmem),
        scratch_shapes=[
            pltpu.VMEM(chunk_grid + (WIDE,), BF16),
            pltpu.VMEM(chunk_grid + (WIDE,), BF16),
            pltpu.VMEM((2, FEAT, HID), BF16),
            pltpu.VMEM((SEQ, FEAT), BF16),
            pltpu.VMEM((FEAT, SEQ), BF16),
            pltpu.VMEM((HEADS * HD, FEAT), BF16),
            pltpu.VMEM((ROWS, HEADS * HD), BF16),
            pltpu.VMEM((QS, HD), BF16),
            pltpu.VMEM((4, ROWS, HD), BF16),
            pltpu.VMEM((4, 8, ROWS, HD), BF16),
            pltpu.VMEM((4, 7, ROWS, HD), BF16),
            pltpu.VMEM((4, 4, 2, ROWS, HD), BF16),
            pltpu.VMEM(chunk_grid + (HEADS * HD,), BF16),
            pltpu.VMEM((3, 4, ROWS, 512), BF16),
            pltpu.VMEM((3, 4, ROWS, 512), BF16),
            pltpu.VMEM((3, ROWS, 512), BF16),
            pltpu.VMEM((3, ROWS, 512), BF16),
            pltpu.VMEM((3, ROWS, 512), BF16),
            pltpu.VMEM((3, ROWS, 512), BF16),
            pltpu.VMEM((ROWS, HEADS * HD), F32),
            pltpu.VMEM((QS, HD), BF16),
            pltpu.VMEM((2, FEAT, HID), BF16),
            pltpu.VMEM((2, FEAT, HID), BF16),
            pltpu.VMEM((2, FEAT, HID), BF16),
            pltpu.VMEM((HD, SEQ), BF16),
            pltpu.VMEM((SEQ, QS), F32),
            pltpu.VMEM((SEQ, QS), BF16),
            pltpu.VMEM((SEQ, QS), BF16),
            pltpu.VMEM(chunk_grid + (HD,), BF16),
            pltpu.VMEM(chunk_grid + (HD,), BF16),
            pltpu.VMEM((3, 4, CUT, HD), BF16),
            pltpu.VMEM((3, 4, ROWS - CUT, HD), BF16),
            pltpu.VMEM((3, 4, ROWS, HD), BF16),
            pltpu.VMEM((3, CUT, HD), BF16),
            pltpu.VMEM((3, ROWS - CUT, HD), BF16),
            pltpu.VMEM((3, ROWS, HD), BF16),
            pltpu.VMEM((3, CUT, HD), BF16),
            pltpu.VMEM((3, ROWS - CUT, HD), BF16),
            pltpu.VMEM((3, ROWS, HD), BF16),
            pltpu.SemaphoreType.DMA((N_GROUPS,)),
            pltpu.SemaphoreType.DMA((N_GROUPS,)),
            pltpu.SemaphoreType.DMA((11,)),
        ],
        compiler_params=pltpu.CompilerParams(
            collective_id=0, has_side_effects=True, vmem_limit_bytes=56 * 1024 * 1024
        ),
    )(
        ffn_input,
        gate_act,
        up_act,
        hidden_grad,
        stream_grad.reshape(16, ROWS, FEAT),
        w_gate,
        w_up,
        gate_keep,
        up_keep,
        w_out,
        queries,
        keys,
        values,
    )
    return pl.pallas_call(
        hand_on,
        out_shape=out_shape,
        in_specs=[hbm] * 5,
        out_specs=(hbm,) * 5,
        scratch_shapes=[pltpu.VMEM(shape.shape, BF16) for shape in out_shape]
        + [pltpu.SemaphoreType.DMA((2 * PARTS + 3,))] * 2,
        compiler_params=pltpu.CompilerParams(vmem_limit_bytes=60 * 1024 * 1024),
    )(*results)


def solution(mesh):
    placed = (
        P("dp", None, "row"),
        P("dp", "row", "col"),
        P("dp", "row", "col"),
        P("dp", "row", "col"),
        P("dp", None, "row"),
        P("row", "col"),
        P("row", "col"),
        P("row", "col"),
        P("row", "col"),
        P("col", "row"),
        P("dp", "row", "col"),
        P("dp", "row", "col"),
        P("dp", "row", "col"),
    )
    return jax.shard_map(
        on_device,
        mesh=mesh,
        in_specs=placed,
        out_specs=(
            P("row", "col"),
            P("row", "col"),
            P("dp", "row", "col"),
            P("dp", "row", "col"),
            P("dp", "row", "col"),
        ),
        check_vma=False,
    )
```

```python
import math

import jax
import jax.numpy as jnp
from jax import lax
from jax.experimental import pallas as pl
from jax.experimental.pallas import tpu as pltpu
from jax.sharding import PartitionSpec as P

MESH = pl.DeviceIdType.MESH
F32 = jnp.float32
BF16 = jnp.bfloat16

ROWS = 80
PARTS = 4
HID = 1792
WIDE = HID + 128
HALF = 1024
FEAT = 256
SEQ = 1280
HEADS = 8
HD = 128
QS = HEADS * ROWS
SCALE = 1.0 / math.sqrt(HD)
NEGATIVE_FILL = -1e30
N_GROUPS = 46
OFFSETS = (-1, 1, 2)

QUARTERS = (
    ((0, 0), (0, -1), (-1, 0), (-1, -1)),
    ((0, 1), (1, 0), (-1, 1), (1, -1)),
    ((0, 2), (2, 0), (1, 2), (2, 1)),
    ((1, 1), (-1, 2), (2, -1), (2, 2)),
)
EARLY = {2: ((0, 2), (1, 3)), 3: ((0, 1), (0, 2))}
LATE = {2: ((1, 3), (0, 2)), 3: ((2, 3), (1, 3))}


def pick(table, j):
    total = 0
    for k, value in enumerate(table):
        total = total + value * (1 - lax.div(lax.rem(j + (4 - k), 4) + 3, 4))
    return total


def nt(left, right):
    return lax.dot_general(left, right, (((1,), (1,)), ((), ())), preferred_element_type=F32)


def nn(left, right):
    return lax.dot_general(left, right, (((1,), (0,)), ((), ())), preferred_element_type=F32)


def kernel(
    ffn_hbm,
    gate_ref,
    up_ref,
    hidden_ref,
    stream_hbm,
    wg_hbm,
    wu_hbm,
    gk_ref,
    uk_ref,
    wo_hbm,
    q_hbm,
    k_ref,
    v_ref,
    gw_hbm,
    uw_hbm,
    dq_ref,
    dk_ref,
    dv_ref,
    ga,
    ua,
    w_eff,
    ffn_v,
    ffn_t,
    wout_v,
    q_v,
    q_s,
    stream_v,
    early,
    zs,
    zr,
    strm,
    hp,
    ra,
    rb,
    ha,
    hb,
    ra2,
    rb2,
    g_own,
    g_s,
    w_send,
    w_recv,
    w_out_v,
    k_t,
    v_t,
    out_t,
    p_f,
    p_low,
    ds_s,
    kt_s,
    vt_s,
    kt_r,
    vt_r,
    kt2_s,
    vt2_s,
    kt2_r,
    vt2_r,
    send_sem,
    recv_sem,
    local_sem,
):
    row = lax.axis_index("row")
    z = lax.axis_index("col")
    core = lax.axis_index("dp")
    y, x = row // 4, row % 4

    def ring(v, off):
        return lax.rem(v + (off + 4), 4)

    def dev(axis, off):
        if axis == "x":
            return {"row": y * 4 + ring(x, off)}
        return {"row": ring(y, off) * 4 + x}

    groups = []

    class Group:
        def __init__(self, size):
            self.i, self.size = len(groups), size
            groups.append(self)

        def copy(self, src, dst, device):
            return pltpu.make_async_remote_copy(
                src_ref=src,
                dst_ref=dst,
                send_sem=send_sem.at[self.i],
                recv_sem=recv_sem.at[self.i],
                device_id=device,
                device_id_type=MESH,
            )

        def send(self, src, dst, device):
            self.copy(src, dst, device).start()

        def wait_recv(self):
            self.copy(self.size, self.size, {"dp": 1 - core}).wait_recv()

        def wait_send(self):
            self.copy(self.size, self.size, {"dp": 1 - core}).wait_send()

    barrier = pltpu.get_barrier_semaphore()
    partners = [dev("x", o) for o in OFFSETS] + [dev("y", o) for o in OFFSETS]
    partners += [{"col": lax.rem(z + o, 8)} for o in range(1, 8)] + [{"dp": 1 - core}]
    for partner in partners:
        pl.semaphore_signal(barrier, inc=1, device_id=partner, device_id_type=MESH)

    def fetch(i, src, dst):
        copy = pltpu.make_async_copy(src, dst, local_sem.at[i])
        copy.start()
        return copy

    def place(chunk):
        dy, dx = chunk
        return lax.rem(y + dy + 4, 4), lax.rem(x + dx + 4, 4)

    mine = []
    for quarter in QUARTERS:
        mine.append(place([pick([chunk[i] for chunk in quarter], z // 2) for i in range(2)]))
    side = lax.rem(z, 2)
    side_cols = pl.ds(pl.multiple_of(side * HD, HD), HD)
    get_wg = fetch(0, wg_hbm, w_eff.at[0])
    get_wu = fetch(1, wu_hbm, w_eff.at[1])
    get_ffn = fetch(2, ffn_hbm.at[0], ffn_v)
    get_wo = fetch(3, wo_hbm, wout_v)
    get_q = fetch(4, q_hbm.at[0], q_v)
    get_st = [
        fetch(5 + b, stream_hbm.at[mine[b][0] * 4 + mine[b][1], :, side_cols], stream_v.at[b])
        for b in range(4)
    ]

    def act_step(i, _):
        cols = pl.ds(pl.multiple_of(i * 128, 128), 128)
        gate_f = gate_ref[0, :, cols].astype(F32)
        hidden_f = hidden_ref[0, :, cols].astype(F32)
        sigma = jax.nn.sigmoid(gate_f)
        ua[y, x, :, cols] = (hidden_f * gate_f * sigma).astype(BF16)
        ga[y, x, :, cols] = (
            hidden_f * up_ref[0, :, cols].astype(F32) * sigma * (1.0 + gate_f * (1.0 - sigma))
        ).astype(BF16)
        return 0

    lax.fori_loop(0, HID // 128, act_step, 0)
    ga[y, x, :, HID:] = k_ref[0]
    ua[y, x, :, HID:] = v_ref[0]

    pl.semaphore_wait(barrier, len(partners))

    arrays = ((ga, "x", "y"), (ua, "y", "x"))

    def at(n, first, second):
        arr, p, _ = arrays[n]
        if p == "x":
            return arr.at[ring(y, second), ring(x, first)]
        return arr.at[ring(y, first), ring(x, second)]

    two_chunks = ga.at[0, 0:2]
    along = {(n, d): Group(at(n, 0, 0)) for n in range(2) for d in (1, -1)}
    relay = [Group(at(n, 2, 0)) for n in range(2)]
    across = {(n, first): Group(two_chunks) for n in range(2) for first in (0, -1, 1, 2)}
    far = {(n, part): Group(two_chunks) for n in range(2) for part in range(2)}

    def spread(n, first):
        block = at(n, first, 0)
        for d in (1, -1):
            across[n, first].send(block, block, dev(arrays[n][2], d))

    for n in range(2):
        for d in (1, -1):
            along[n, d].send(at(n, 0, 0), at(n, 0, 0), dev(arrays[n][1], d))
    for n in range(2):
        spread(n, 0)

    for n, (get, keep) in enumerate(((get_wg, gk_ref), (get_wu, uk_ref))):
        get.wait()

        def mask_step(j, _, n=n, keep=keep):
            cols = pl.ds(pl.multiple_of(j * 128, 128), 128)
            for i in range(2):
                rows = slice(i * 128, (i + 1) * 128)
                tile = w_eff[n, rows, cols].astype(F32) * keep[i, j].astype(F32)
                w_eff[n, rows, cols] = tile.astype(BF16)
            return 0

        lax.fori_loop(0, HID // 128, mask_step, 0)

    for d in (1, -1):
        for n in range(2):
            along[n, d].wait_recv()
            cols = slice(0, HALF) if d == 1 else slice(HALF, WIDE)
            part = at(n, -d, 0).at[:, cols]
            relay[n].send(part, part, dev(arrays[n][1], d))
            spread(n, -d)

    get_ffn.wait()

    def transpose_step(i, _):
        rows = pl.ds(pl.multiple_of(i * 256, 256), 256)
        ffn_t[:, rows] = ffn_v[rows, :].T
        return 0

    lax.fori_loop(0, SEQ // 256, transpose_step, 0)
    get_q.wait()
    for h in range(HEADS):
        q_s[h * ROWS : (h + 1) * ROWS, :] = q_v[:, h * HD : (h + 1) * HD]

    for n in range(2):
        relay[n].wait_recv()
        spread(n, 2)

    col_sum = [Group(zr.at[b]) for b in range(4)]
    col_all = [Group(zr.at[b]) for b in range(4)]

    def terms(n, chunks):
        spots = [place(c) for c in chunks]
        rows = jnp.concatenate([arrays[n][0][yc, xc, :, 0:HID] for yc, xc in spots], axis=0)
        return nt(rows, w_eff[n])

    def send_sums(b, i, total):
        for j in range(2):
            zs[b, i * 2 + j] = total[:, j * HD : (j + 1) * HD].astype(BF16)

    def scatter_col(b):
        for off in range(1, 8):
            to = lax.rem(z + off, 8)
            col_sum[b].send(zs.at[b, to], zr.at[b, off - 1], {"col": to})

    def input_terms(b):
        total = terms(0, QUARTERS[b]) + terms(1, QUARTERS[b])
        for i in range(4):
            send_sums(b, i, total[i * ROWS : (i + 1) * ROWS])
        scatter_col(b)

    def early_terms(b):
        for n in range(2):
            early[n] = terms(n, [QUARTERS[b][i] for i in EARLY[b][n]])

    def late_terms(b):
        late = [terms(n, [QUARTERS[b][i] for i in LATE[b][n]]) for n in range(2)]
        for i in range(4):
            total = 0.0
            for n in range(2):
                if i in EARLY[b][n]:
                    j = EARLY[b][n].index(i) * ROWS
                    total += early[n, j : j + ROWS, :]
                else:
                    j = LATE[b][n].index(i) * ROWS
                    total += late[n][j : j + ROWS, :]
            send_sums(b, i, total)
        scatter_col(b)

    def gather_col(b):
        col_sum[b].wait_recv()
        get_st[b].wait()
        total = zs[b, z].astype(F32)
        for j in range(7):
            total += zr[b, j].astype(F32)
        yc, xc = mine[b]
        strm[yc, xc, side] = (stream_v[b].astype(F32) + total).astype(BF16)
        block = strm.at[yc, xc, side]
        for off in range(1, 8):
            col_all[b].send(block, block, {"col": lax.rem(z + off, 8)})

    first_a = {dy: Group(ra2) for dy in (0, -1, 1, 2)}
    first_b = {dx: Group(rb2) for dx in (0, -1, 1, 2)}

    def head_terms(b, at_once=True):
        col_all[b].wait_recv()
        spots = [place(c) for c in QUARTERS[b]]
        total = jnp.concatenate(
            [
                jnp.concatenate([strm[yc, xc, j] for yc, xc in spots], axis=0) for j in range(2)
            ],
            axis=1,
        )

        def step(t, _):
            cols = pl.ds(pl.multiple_of(t * 256, 256), 256)
            part = nt(total, wout_v[cols, :]).astype(BF16)
            for i, (yc, xc) in enumerate(spots):
                hp[yc, xc, :, cols] = part[i * ROWS : (i + 1) * ROWS, :]
            return 0

        lax.fori_loop(0, 2, step, 0)
        if at_once:
            send_a(b)
        lax.fori_loop(2, 4, step, 0)
        if at_once:
            send_b(b)

    def send_a(b):
        for dy, dx in QUARTERS[b][::-1]:
            yc, xc = place((dy, dx))
            if dx != 0:
                first_a[dy].send(
                    hp.at[yc, xc, :, 0:512], ra.at[OFFSETS.index(dx), yc], dev("x", dx)
                )

    def send_b(b):
        for dy, dx in QUARTERS[b][::-1]:
            yc, xc = place((dy, dx))
            if dy != 0:
                first_b[dx].send(
                    hp.at[yc, xc, :, 512:1024], rb.at[OFFSETS.index(dy), xc], dev("y", dy)
                )

    for first, d, part in ((0, 1, 0), (-1, 1, 1), (1, -1, 0), (2, -1, 1)):
        for n in range(2):
            across[n, first].wait_recv()
            block = at(n, first, -d)
            far[n, part].send(block, block, dev(arrays[n][2], d))
        if first == -1:
            input_terms(0)
        if first == 1:
            input_terms(1)

    gather_col(0)
    gather_col(1)
    get_wo.wait()
    head_terms(0, at_once=False)
    for n in range(2):
        far[n, 0].wait_recv()
    input_terms(2)
    for n in range(2):
        far[n, 1].wait_recv()
    input_terms(3)
    send_a(0)
    send_b(0)
    gather_col(2)

    def wgrad(n):
        arr = arrays[n][0]

        def step(t, _):
            cols = pl.ds(pl.multiple_of(t * 256, 256), 256)
            tokens = arr[:, :, :, cols].reshape(SEQ, 256)
            w_send[n, :, cols] = nn(ffn_t[...], tokens).astype(BF16)
            return 0

        lax.fori_loop(0, HID // 256, step, 0)
        pair[n].send(w_send.at[n], w_recv.at[n], {"dp": 1 - core})

    pair = [Group(w_recv.at[n]) for n in range(2)]
    head_terms(1)
    wgrad(0)
    gather_col(3)
    head_terms(2)
    head_terms(3)
    wgrad(1)

    k_t[...] = ga[:, :, :, HID:].reshape(SEQ, HD).T
    v_t[...] = ua[:, :, :, HID:].reshape(SEQ, HD).T

    def softmax_step(t, _):
        cols = pl.ds(pl.multiple_of(t * 128, 128), 128)
        scores = nt(ga[:, :, :, HID:].reshape(SEQ, HD), q_s[cols, :]) * SCALE
        lane = lax.broadcasted_iota(jnp.int32, (1, 128), 1) + t * 128
        head = jnp.zeros_like(lane)
        for h in range(1, HEADS):
            head += (lane >= h * ROWS).astype(jnp.int32)
        query_pos = lane - head * ROWS + row * ROWS
        key_pos = lax.broadcasted_iota(jnp.int32, (SEQ, 128), 0)
        scores = jnp.where(key_pos <= query_pos, scores, NEGATIVE_FILL)
        weight = jnp.exp(scores - jnp.max(scores, axis=0, keepdims=True))
        probs = weight * (1.0 / jnp.sum(weight, axis=0, keepdims=True))
        p_f[:, cols] = probs
        p_low[:, cols] = probs.astype(BF16)
        out_t[:, cols] = nn(v_t[...], p_low[:, cols])
        return 0

    lax.fori_loop(0, QS // 128, softmax_step, 0)

    second_a, second_b = Group(ra2), Group(rb2)
    for off in (2, -1, 1, 0):
        first_a[off].wait_recv()
        first_b[off].wait_recv()
        yc, xc = ring(y, off), ring(x, off)
        total_a = hp[yc, x, :, 0:512].astype(F32)
        total_b = hp[y, xc, :, 512:1024].astype(F32)
        for k in range(3):
            total_a += ra[k, yc].astype(F32)
            total_b += rb[k, xc].astype(F32)
        if off == 0:
            g_own[:, 0:512] = total_a
            g_own[:, 512:1024] = total_b
        else:
            k = OFFSETS.index(off)
            ha[k] = total_a.astype(BF16)
            hb[k] = total_b.astype(BF16)
            second_a.send(ha.at[k], ra2.at[k], dev("y", off))
            second_b.send(hb.at[k], rb2.at[k], dev("x", off))

    put = []
    for n, (keep, out) in enumerate(((gk_ref, gw_hbm), (uk_ref, uw_hbm))):
        pair[n].wait_recv()

        def sum_step(j, _, n=n, keep=keep):
            cols = pl.ds(pl.multiple_of(j * 128, 128), 128)
            for i in range(2):
                rows = slice(i * 128, (i + 1) * 128)
                total = w_send[n, rows, cols].astype(F32) + w_recv[n, rows, cols].astype(F32)
                w_out_v[n, rows, cols] = (total * keep[i, j].astype(F32)).astype(BF16)
            return 0

        lax.fori_loop(0, HID // 128, sum_step, 0)
        put.append(fetch(9 + n, w_out_v.at[n], out))

    second_a.wait_recv()
    second_b.wait_recv()
    for h in range(HEADS):
        cols = slice(h * HD, (h + 1) * HD)
        total = g_own[:, cols]
        buf = ra2 if h < 4 else rb2
        low = slice((h % 4) * HD, (h % 4 + 1) * HD)
        for k in range(3):
            total += buf[k, :, low].astype(F32)
        g_s[h * ROWS : (h + 1) * ROWS, :] = total.astype(BF16)

    val1, val2 = Group(vt_r), Group(vt2_r)
    key1, key2 = Group(kt_r), Group(kt2_r)
    delta = jnp.sum(out_t[...] * g_s[...].astype(F32).T, axis=0, keepdims=True)
    for off in (2, -1, 1, 0):
        yc = ring(y, off)
        rows = pl.ds(pl.multiple_of(yc * 320, 320), 320)
        prob_grad = nt(ua[yc, :, :, HID:].reshape(320, HD), g_s[...])
        part = nn(p_low[rows, :], g_s[...]).astype(BF16)
        for i in range(4):
            vt_s[yc, i] = part[i * ROWS : (i + 1) * ROWS, :]
        if off != 0:
            val1.send(vt_s.at[yc], vt_r.at[OFFSETS.index(off)], dev("y", off))
        score = (p_f[rows, :] * (prob_grad - delta) * SCALE).astype(BF16)
        ds_s[rows, :] = score
        part = nn(score, q_s[...]).astype(BF16)
        for i in range(4):
            kt_s[yc, i] = part[i * ROWS : (i + 1) * ROWS, :]
        for k, o in enumerate(OFFSETS):
            xc = ring(x, o)
            key1.send(kt_s.at[yc, xc], kt_r.at[k, yc], dev("x", o))

    def q_step(t, _):
        cols = pl.ds(pl.multiple_of(t * 128, 128), 128)
        q_s[cols, :] = nn(k_t[...], ds_s[:, cols]).T.astype(BF16)
        return 0

    lax.fori_loop(0, QS // 128, q_step, 0)
    for h in range(HEADS):
        dq_ref[0, :, h * HD : (h + 1) * HD] = q_s[h * ROWS : (h + 1) * ROWS, :]

    def add_up(first, own, recv, buf, axis, keep_at, second, landing):
        first.wait_recv()
        for k, o in enumerate(OFFSETS):
            spot = ring(keep_at, o)
            total = own(spot).astype(F32)
            for j in range(3):
                total += recv[j, spot].astype(F32)
            buf[k] = total.astype(BF16)
            second.send(buf.at[k], landing.at[k], dev(axis, o))
        total = own(keep_at).astype(F32)
        for j in range(3):
            total += recv[j, keep_at].astype(F32)
        return total

    val_own = add_up(val1, lambda i: vt_s[y, i], vt_r, vt2_s, "x", x, val2, vt2_r)
    key_own = add_up(key1, lambda i: kt_s[i, x], kt_r, kt2_s, "y", y, key2, kt2_r)
    for own, second, landing, out in (
        (val_own, val2, vt2_r, dv_ref),
        (key_own, key2, kt2_r, dk_ref),
    ):
        second.wait_recv()
        for k in range(3):
            own += landing[k].astype(F32)
        out[0] = own.astype(BF16)

    for group in groups:
        group.wait_send()
    for copy in put:
        copy.wait()


def hand_on(*refs):
    sources, targets, through, (get_sem, put_sem) = refs[:5], refs[5:10], refs[10:15], refs[15:]
    parts = []
    for n in range(5):
        for i in range(PARTS if n < 2 else 1):
            rows = pl.ds(i * (FEAT // PARTS), FEAT // PARTS) if n < 2 else 0
            parts.append([ref.at[rows] for ref in (sources[n], through[n], targets[n])])
    gets = [
        pltpu.make_async_copy(part[0], part[1], get_sem.at[i]) for i, part in enumerate(parts)
    ]
    puts = [
        pltpu.make_async_copy(part[1], part[2], put_sem.at[i]) for i, part in enumerate(parts)
    ]
    for get in gets:
        get.start()
    for get, put in zip(gets, puts):
        get.wait()
        put.start()
    for put in puts:
        put.wait()


def on_device(
    ffn_input,
    gate_act,
    up_act,
    hidden_grad,
    stream_grad,
    w_gate,
    w_up,
    gate_keep,
    up_keep,
    w_out,
    queries,
    keys,
    values,
):
    hbm = pl.BlockSpec(memory_space=pl.ANY)
    vmem = pl.BlockSpec(memory_space=pltpu.VMEM)
    smem = pl.BlockSpec(memory_space=pltpu.SMEM)
    chunk_grid = (4, 4, ROWS)
    out_shape = (
        jax.ShapeDtypeStruct((FEAT, HID), BF16),
        jax.ShapeDtypeStruct((FEAT, HID), BF16),
        jax.ShapeDtypeStruct((1, ROWS, HEADS * HD), BF16),
        jax.ShapeDtypeStruct((1, ROWS, HD), BF16),
        jax.ShapeDtypeStruct((1, ROWS, HD), BF16),
    )
    results = pl.pallas_call(
        kernel,
        out_shape=out_shape,
        in_specs=[hbm, vmem, vmem, vmem, hbm, hbm, hbm, smem, smem, hbm, hbm, vmem, vmem],
        out_specs=(hbm, hbm, vmem, vmem, vmem),
        scratch_shapes=[
            pltpu.VMEM(chunk_grid + (WIDE,), BF16),
            pltpu.VMEM(chunk_grid + (WIDE,), BF16),
            pltpu.VMEM((2, FEAT, HID), BF16),
            pltpu.VMEM((SEQ, FEAT), BF16),
            pltpu.VMEM((FEAT, SEQ), BF16),
            pltpu.VMEM((HEADS * HD, FEAT), BF16),
            pltpu.VMEM((ROWS, HEADS * HD), BF16),
            pltpu.VMEM((QS, HD), BF16),
            pltpu.VMEM((4, ROWS, HD), BF16),
            pltpu.VMEM((2, 2 * ROWS, FEAT), F32),
            pltpu.VMEM((4, 8, ROWS, HD), BF16),
            pltpu.VMEM((4, 7, ROWS, HD), BF16),
            pltpu.VMEM((4, 4, 2, ROWS, HD), BF16),
            pltpu.VMEM(chunk_grid + (HEADS * HD,), BF16),
            pltpu.VMEM((3, 4, ROWS, 512), BF16),
            pltpu.VMEM((3, 4, ROWS, 512), BF16),
            pltpu.VMEM((3, ROWS, 512), BF16),
            pltpu.VMEM((3, ROWS, 512), BF16),
            pltpu.VMEM((3, ROWS, 512), BF16),
            pltpu.VMEM((3, ROWS, 512), BF16),
            pltpu.VMEM((ROWS, HEADS * HD), F32),
            pltpu.VMEM((QS, HD), BF16),
            pltpu.VMEM((2, FEAT, HID), BF16),
            pltpu.VMEM((2, FEAT, HID), BF16),
            pltpu.VMEM((2, FEAT, HID), BF16),
            pltpu.VMEM((HD, SEQ), BF16),
            pltpu.VMEM((HD, SEQ), BF16),
            pltpu.VMEM((HD, QS), F32),
            pltpu.VMEM((SEQ, QS), F32),
            pltpu.VMEM((SEQ, QS), BF16),
            pltpu.VMEM((SEQ, QS), BF16),
            pltpu.VMEM(chunk_grid + (HD,), BF16),
            pltpu.VMEM(chunk_grid + (HD,), BF16),
            pltpu.VMEM((3, 4, ROWS, HD), BF16),
            pltpu.VMEM((3, 4, ROWS, HD), BF16),
            pltpu.VMEM((3, ROWS, HD), BF16),
            pltpu.VMEM((3, ROWS, HD), BF16),
            pltpu.VMEM((3, ROWS, HD), BF16),
            pltpu.VMEM((3, ROWS, HD), BF16),
            pltpu.SemaphoreType.DMA((N_GROUPS,)),
            pltpu.SemaphoreType.DMA((N_GROUPS,)),
            pltpu.SemaphoreType.DMA((11,)),
        ],
        compiler_params=pltpu.CompilerParams(
            collective_id=0, has_side_effects=True, vmem_limit_bytes=56 * 1024 * 1024
        ),
    )(
        ffn_input,
        gate_act,
        up_act,
        hidden_grad,
        stream_grad.reshape(16, ROWS, FEAT),
        w_gate,
        w_up,
        gate_keep,
        up_keep,
        w_out,
        queries,
        keys,
        values,
    )
    return pl.pallas_call(
        hand_on,
        out_shape=out_shape,
        in_specs=[hbm] * 5,
        out_specs=(hbm,) * 5,
        scratch_shapes=[pltpu.VMEM(shape.shape, BF16) for shape in out_shape]
        + [pltpu.SemaphoreType.DMA((2 * PARTS + 3,))] * 2,
        compiler_params=pltpu.CompilerParams(vmem_limit_bytes=60 * 1024 * 1024),
    )(*results)


def solution(mesh):
    placed = (
        P("dp", None, "row"),
        P("dp", "row", "col"),
        P("dp", "row", "col"),
        P("dp", "row", "col"),
        P("dp", None, "row"),
        P("row", "col"),
        P("row", "col"),
        P("row", "col"),
        P("row", "col"),
        P("col", "row"),
        P("dp", "row", "col"),
        P("dp", "row", "col"),
        P("dp", "row", "col"),
    )
    return jax.shard_map(
        on_device,
        mesh=mesh,
        in_specs=placed,
        out_specs=(
            P("row", "col"),
            P("row", "col"),
            P("dp", "row", "col"),
            P("dp", "row", "col"),
            P("dp", "row", "col"),
        ),
        check_vma=False,
    )
```

```python
import math

import jax
import jax.numpy as jnp
from jax import lax
from jax.experimental import pallas as pl
from jax.experimental.pallas import tpu as pltpu
from jax.sharding import PartitionSpec as P

MESH = pl.DeviceIdType.MESH
F32 = jnp.float32
BF16 = jnp.bfloat16

ROWS = 80
PARTS = 4
HID = 1792
HALF = 896
FEAT = 256
SEQ = 1280
HEADS = 8
HD = 128
QS = HEADS * ROWS
SCALE = 1.0 / math.sqrt(HD)
NEGATIVE_FILL = -1e30
N_GROUPS = 46
OFFSETS = (-1, 1, 2)

QUARTERS = (
    ((0, 0), (0, -1), (-1, 0), (-1, -1)),
    ((0, 1), (1, 0), (-1, 1), (1, -1)),
    ((0, 2), (2, 0), (1, 2), (2, 1)),
    ((1, 1), (-1, 2), (2, -1), (2, 2)),
)

def pick(table, j):
    total = 0
    for k, value in enumerate(table):
        total = total + value * (1 - lax.div(lax.rem(j + (4 - k), 4) + 3, 4))
    return total


def nt(left, right):
    return lax.dot_general(left, right, (((1,), (1,)), ((), ())), preferred_element_type=F32)


def nn(left, right):
    return lax.dot_general(left, right, (((1,), (0,)), ((), ())), preferred_element_type=F32)


def kernel(
    ffn_hbm,
    gate_ref,
    up_ref,
    hidden_ref,
    stream_hbm,
    wg_hbm,
    wu_hbm,
    gk_ref,
    uk_ref,
    wo_hbm,
    q_hbm,
    k_ref,
    v_ref,
    gw_hbm,
    uw_hbm,
    dq_ref,
    dk_ref,
    dv_ref,
    ga,
    ua,
    k_all,
    v_all,
    w_eff,
    ffn_v,
    ffn_t,
    wout_v,
    q_v,
    q_s,
    stream_v,
    zs,
    zr,
    strm,
    hp,
    ra,
    rb,
    ha,
    hb,
    ra2,
    rb2,
    g_own,
    g_s,
    w_send,
    w_recv,
    w_out_v,
    k_t,
    v_t,
    out_t,
    p_f,
    p_low,
    ds_s,
    kt_s,
    vt_s,
    kt_r,
    vt_r,
    kt2_s,
    vt2_s,
    kt2_r,
    vt2_r,
    send_sem,
    recv_sem,
    local_sem,
):
    row = lax.axis_index("row")
    z = lax.axis_index("col")
    core = lax.axis_index("dp")
    y, x = row // 4, row % 4

    def ring(v, off):
        return lax.rem(v + (off + 4), 4)

    def dev(axis, off):
        if axis == "x":
            return {"row": y * 4 + ring(x, off)}
        return {"row": ring(y, off) * 4 + x}

    groups = []

    class Group:
        def __init__(self, size):
            self.i, self.size = len(groups), size
            groups.append(self)

        def copy(self, src, dst, device):
            return pltpu.make_async_remote_copy(
                src_ref=src,
                dst_ref=dst,
                send_sem=send_sem.at[self.i],
                recv_sem=recv_sem.at[self.i],
                device_id=device,
                device_id_type=MESH,
            )

        def send(self, src, dst, device):
            self.copy(src, dst, device).start()

        def wait_recv(self):
            self.copy(self.size, self.size, {"dp": 1 - core}).wait_recv()

        def wait_send(self):
            self.copy(self.size, self.size, {"dp": 1 - core}).wait_send()

    barrier = pltpu.get_barrier_semaphore()
    partners = [dev("x", o) for o in OFFSETS] + [dev("y", o) for o in OFFSETS]
    partners += [{"col": lax.rem(z + o, 8)} for o in range(1, 8)] + [{"dp": 1 - core}]
    for partner in partners:
        pl.semaphore_signal(barrier, inc=1, device_id=partner, device_id_type=MESH)

    def fetch(i, src, dst):
        copy = pltpu.make_async_copy(src, dst, local_sem.at[i])
        copy.start()
        return copy

    def place(chunk):
        dy, dx = chunk
        return lax.rem(y + dy + 4, 4), lax.rem(x + dx + 4, 4)

    mine = []
    for quarter in QUARTERS:
        mine.append(place([pick([chunk[i] for chunk in quarter], z // 2) for i in range(2)]))
    side = lax.rem(z, 2)
    side_cols = pl.ds(pl.multiple_of(side * HD, HD), HD)
    get_wg = fetch(0, wg_hbm, w_eff.at[0])
    get_wu = fetch(1, wu_hbm, w_eff.at[1])
    get_ffn = fetch(2, ffn_hbm.at[0], ffn_v)
    get_wo = fetch(3, wo_hbm, wout_v)
    get_q = fetch(4, q_hbm.at[0], q_v)
    get_st = [
        fetch(5 + b, stream_hbm.at[mine[b][0] * 4 + mine[b][1], :, side_cols], stream_v.at[b])
        for b in range(4)
    ]

    def act_step(i, _):
        cols = pl.ds(pl.multiple_of(i * 128, 128), 128)
        gate_f = gate_ref[0, :, cols].astype(F32)
        hidden_f = hidden_ref[0, :, cols].astype(F32)
        sigma = jax.nn.sigmoid(gate_f)
        ua[y, x, :, cols] = (hidden_f * gate_f * sigma).astype(BF16)
        ga[y, x, :, cols] = (
            hidden_f * up_ref[0, :, cols].astype(F32) * sigma * (1.0 + gate_f * (1.0 - sigma))
        ).astype(BF16)
        return 0

    lax.fori_loop(0, HID // 128, act_step, 0)
    k_all[y, x] = k_ref[0]
    v_all[y, x] = v_ref[0]

    pl.semaphore_wait(barrier, len(partners))

    arrays = ((ga, "x", "y"), (ua, "y", "x"))

    def at(n, first, second):
        arr, p, _ = arrays[n]
        if p == "x":
            return arr.at[ring(y, second), ring(x, first)]
        return arr.at[ring(y, first), ring(x, second)]

    two_chunks = ga.at[0, 0:2]
    along = {(n, d): Group(at(n, 0, 0)) for n in range(2) for d in (1, -1)}
    relay = [Group(at(n, 2, 0)) for n in range(2)]
    across = {(n, first): Group(two_chunks) for n in range(2) for first in (0, -1, 1, 2)}
    far = {(n, part): Group(two_chunks) for n in range(2) for part in range(2)}

    def spread(n, first):
        block = at(n, first, 0)
        for d in (1, -1):
            across[n, first].send(block, block, dev(arrays[n][2], d))

    for n in range(2):
        for d in (1, -1):
            along[n, d].send(at(n, 0, 0), at(n, 0, 0), dev(arrays[n][1], d))
    for n in range(2):
        spread(n, 0)

    keys1, values1 = Group(k_all.at[0, 0:3]), Group(v_all.at[0, 0:3])
    keys2, values2 = Group(k_all.at[0:3]), Group(v_all.at[0:3])
    for o in OFFSETS:
        keys1.send(k_all.at[y, x], k_all.at[y, x], dev("x", o))
        values1.send(v_all.at[y, x], v_all.at[y, x], dev("y", o))

    for n, (get, keep) in enumerate(((get_wg, gk_ref), (get_wu, uk_ref))):
        get.wait()

        def mask_step(j, _, n=n, keep=keep):
            cols = pl.ds(pl.multiple_of(j * 128, 128), 128)
            for i in range(2):
                rows = slice(i * 128, (i + 1) * 128)
                tile = w_eff[n, rows, cols].astype(F32) * keep[i, j].astype(F32)
                w_eff[n, rows, cols] = tile.astype(BF16)
            return 0

        lax.fori_loop(0, HID // 128, mask_step, 0)

    for d in (1, -1):
        for n in range(2):
            along[n, d].wait_recv()
            cols = slice(0, HALF) if d == 1 else slice(HALF, HID)
            part = at(n, -d, 0).at[:, cols]
            relay[n].send(part, part, dev(arrays[n][1], d))
            spread(n, -d)

    get_ffn.wait()

    def transpose_step(i, _):
        rows = pl.ds(pl.multiple_of(i * 256, 256), 256)
        ffn_t[:, rows] = ffn_v[rows, :].T
        return 0

    lax.fori_loop(0, SEQ // 256, transpose_step, 0)
    get_q.wait()
    for h in range(HEADS):
        q_s[h * ROWS : (h + 1) * ROWS, :] = q_v[:, h * HD : (h + 1) * HD]

    for n in range(2):
        relay[n].wait_recv()
        spread(n, 2)

    col_sum = [Group(zr.at[b]) for b in range(4)]
    col_all = [Group(zr.at[b]) for b in range(4)]

    def terms(n, chunks):
        spots = [place(c) for c in chunks]
        rows = jnp.concatenate([arrays[n][0][yc, xc, :, :] for yc, xc in spots], axis=0)
        return nt(rows, w_eff[n])

    def send_sums(b, i, total):
        for j in range(2):
            zs[b, i * 2 + j] = total[:, j * HD : (j + 1) * HD].astype(BF16)

    def scatter_col(b):
        for off in range(1, 8):
            to = lax.rem(z + off, 8)
            col_sum[b].send(zs.at[b, to], zr.at[b, off - 1], {"col": to})

    def input_terms(b):
        total = terms(0, QUARTERS[b]) + terms(1, QUARTERS[b])
        for i in range(4):
            send_sums(b, i, total[i * ROWS : (i + 1) * ROWS])
        scatter_col(b)

    def gather_col(b):
        col_sum[b].wait_recv()
        get_st[b].wait()
        total = zs[b, z].astype(F32)
        for j in range(7):
            total += zr[b, j].astype(F32)
        yc, xc = mine[b]
        strm[yc, xc, side] = (stream_v[b].astype(F32) + total).astype(BF16)
        block = strm.at[yc, xc, side]
        for off in range(1, 8):
            col_all[b].send(block, block, {"col": lax.rem(z + off, 8)})

    first_a = {dy: Group(ra2) for dy in (0, -1, 1, 2)}
    first_b = {dx: Group(rb2) for dx in (0, -1, 1, 2)}

    def head_terms(b, at_once=True):
        col_all[b].wait_recv()
        spots = [place(c) for c in QUARTERS[b]]
        total = jnp.concatenate(
            [
                jnp.concatenate([strm[yc, xc, j] for yc, xc in spots], axis=0) for j in range(2)
            ],
            axis=1,
        )

        def step(t, _):
            cols = pl.ds(pl.multiple_of(t * 256, 256), 256)
            part = nt(total, wout_v[cols, :]).astype(BF16)
            for i, (yc, xc) in enumerate(spots):
                hp[yc, xc, :, cols] = part[i * ROWS : (i + 1) * ROWS, :]
            return 0

        lax.fori_loop(0, 2, step, 0)
        if at_once:
            send_a(b)
        lax.fori_loop(2, 4, step, 0)
        if at_once:
            send_b(b)

    def send_a(b):
        for dy, dx in QUARTERS[b][::-1]:
            yc, xc = place((dy, dx))
            if dx != 0:
                first_a[dy].send(
                    hp.at[yc, xc, :, 0:512], ra.at[OFFSETS.index(dx), yc], dev("x", dx)
                )

    def send_b(b):
        for dy, dx in QUARTERS[b][::-1]:
            yc, xc = place((dy, dx))
            if dy != 0:
                first_b[dx].send(
                    hp.at[yc, xc, :, 512:1024], rb.at[OFFSETS.index(dy), xc], dev("y", dy)
                )

    for first, d, part in ((0, 1, 0), (-1, 1, 1), (1, -1, 0), (2, -1, 1)):
        for n in range(2):
            across[n, first].wait_recv()
            block = at(n, first, -d)
            far[n, part].send(block, block, dev(arrays[n][2], d))
        if first == -1:
            input_terms(0)
        if first == 1:
            input_terms(1)

    gather_col(0)
    gather_col(1)
    get_wo.wait()
    head_terms(0, at_once=False)
    for n in range(2):
        far[n, 0].wait_recv()
    input_terms(2)
    for n in range(2):
        far[n, 1].wait_recv()
    input_terms(3)
    keys1.wait_recv()
    values1.wait_recv()
    for o in OFFSETS:
        keys2.send(k_all.at[y], k_all.at[y], dev("y", o))
        values2.send(v_all.at[:, x], v_all.at[:, x], dev("x", o))
    send_a(0)
    send_b(0)
    gather_col(2)

    def wgrad(n):
        arr = arrays[n][0]

        def step(t, _):
            cols = pl.ds(pl.multiple_of(t * 256, 256), 256)
            tokens = arr[:, :, :, cols].reshape(SEQ, 256)
            w_send[n, :, cols] = nn(ffn_t[...], tokens).astype(BF16)
            return 0

        lax.fori_loop(0, HID // 256, step, 0)
        pair[n].send(w_send.at[n], w_recv.at[n], {"dp": 1 - core})

    pair = [Group(w_recv.at[n]) for n in range(2)]
    head_terms(1)
    wgrad(0)
    gather_col(3)
    head_terms(2)
    head_terms(3)
    wgrad(1)

    keys2.wait_recv()
    values2.wait_recv()
    k_t[...] = k_all[...].reshape(SEQ, HD).T
    v_t[...] = v_all[...].reshape(SEQ, HD).T

    def softmax_step(t, _):
        cols = pl.ds(pl.multiple_of(t * 128, 128), 128)
        scores = nt(k_all[...].reshape(SEQ, HD), q_s[cols, :]) * SCALE
        lane = lax.broadcasted_iota(jnp.int32, (1, 128), 1) + t * 128
        head = jnp.zeros_like(lane)
        for h in range(1, HEADS):
            head += (lane >= h * ROWS).astype(jnp.int32)
        query_pos = lane - head * ROWS + row * ROWS
        key_pos = lax.broadcasted_iota(jnp.int32, (SEQ, 128), 0)
        scores = jnp.where(key_pos <= query_pos, scores, NEGATIVE_FILL)
        weight = jnp.exp(scores - jnp.max(scores, axis=0, keepdims=True))
        probs = weight * (1.0 / jnp.sum(weight, axis=0, keepdims=True))
        p_f[:, cols] = probs
        p_low[:, cols] = probs.astype(BF16)
        out_t[:, cols] = nn(v_t[...], p_low[:, cols])
        return 0

    lax.fori_loop(0, QS // 128, softmax_step, 0)

    second_a, second_b = Group(ra2), Group(rb2)
    for off in (2, -1, 1, 0):
        first_a[off].wait_recv()
        first_b[off].wait_recv()
        yc, xc = ring(y, off), ring(x, off)
        total_a = hp[yc, x, :, 0:512].astype(F32)
        total_b = hp[y, xc, :, 512:1024].astype(F32)
        for k in range(3):
            total_a += ra[k, yc].astype(F32)
            total_b += rb[k, xc].astype(F32)
        if off == 0:
            g_own[:, 0:512] = total_a
            g_own[:, 512:1024] = total_b
        else:
            k = OFFSETS.index(off)
            ha[k] = total_a.astype(BF16)
            hb[k] = total_b.astype(BF16)
            second_a.send(ha.at[k], ra2.at[k], dev("y", off))
            second_b.send(hb.at[k], rb2.at[k], dev("x", off))

    put = []
    for n, (keep, out) in enumerate(((gk_ref, gw_hbm), (uk_ref, uw_hbm))):
        pair[n].wait_recv()

        def sum_step(j, _, n=n, keep=keep):
            cols = pl.ds(pl.multiple_of(j * 128, 128), 128)
            for i in range(2):
                rows = slice(i * 128, (i + 1) * 128)
                total = w_send[n, rows, cols].astype(F32) + w_recv[n, rows, cols].astype(F32)
                w_out_v[n, rows, cols] = (total * keep[i, j].astype(F32)).astype(BF16)
            return 0

        lax.fori_loop(0, HID // 128, sum_step, 0)
        put.append(fetch(9 + n, w_out_v.at[n], out))

    second_a.wait_recv()
    second_b.wait_recv()
    for h in range(HEADS):
        cols = slice(h * HD, (h + 1) * HD)
        total = g_own[:, cols]
        buf = ra2 if h < 4 else rb2
        low = slice((h % 4) * HD, (h % 4 + 1) * HD)
        for k in range(3):
            total += buf[k, :, low].astype(F32)
        g_s[h * ROWS : (h + 1) * ROWS, :] = total.astype(BF16)

    val1, val2 = Group(vt_r), Group(vt2_r)
    key1, key2 = Group(kt_r), Group(kt2_r)
    delta = jnp.sum(out_t[...] * g_s[...].astype(F32).T, axis=0, keepdims=True)
    for off in (2, -1, 1, 0):
        yc = ring(y, off)
        rows = pl.ds(pl.multiple_of(yc * 320, 320), 320)
        prob_grad = nt(v_all[yc].reshape(320, HD), g_s[...])
        part = nn(p_low[rows, :], g_s[...]).astype(BF16)
        for i in range(4):
            vt_s[yc, i] = part[i * ROWS : (i + 1) * ROWS, :]
        if off != 0:
            val1.send(vt_s.at[yc], vt_r.at[OFFSETS.index(off)], dev("y", off))
        score = (p_f[rows, :] * (prob_grad - delta) * SCALE).astype(BF16)
        ds_s[rows, :] = score
        part = nn(score, q_s[...]).astype(BF16)
        for i in range(4):
            kt_s[yc, i] = part[i * ROWS : (i + 1) * ROWS, :]
        for k, o in enumerate(OFFSETS):
            xc = ring(x, o)
            key1.send(kt_s.at[yc, xc], kt_r.at[k, yc], dev("x", o))

    def q_step(t, _):
        cols = pl.ds(pl.multiple_of(t * 128, 128), 128)
        q_s[cols, :] = nn(k_t[...], ds_s[:, cols]).T.astype(BF16)
        return 0

    lax.fori_loop(0, QS // 128, q_step, 0)
    for h in range(HEADS):
        dq_ref[0, :, h * HD : (h + 1) * HD] = q_s[h * ROWS : (h + 1) * ROWS, :]

    def add_up(first, own, recv, buf, axis, keep_at, second, landing):
        first.wait_recv()
        for k, o in enumerate(OFFSETS):
            spot = ring(keep_at, o)
            total = own(spot).astype(F32)
            for j in range(3):
                total += recv[j, spot].astype(F32)
            buf[k] = total.astype(BF16)
            second.send(buf.at[k], landing.at[k], dev(axis, o))
        total = own(keep_at).astype(F32)
        for j in range(3):
            total += recv[j, keep_at].astype(F32)
        return total

    val_own = add_up(val1, lambda i: vt_s[y, i], vt_r, vt2_s, "x", x, val2, vt2_r)
    key_own = add_up(key1, lambda i: kt_s[i, x], kt_r, kt2_s, "y", y, key2, kt2_r)
    for own, second, landing, out in (
        (val_own, val2, vt2_r, dv_ref),
        (key_own, key2, kt2_r, dk_ref),
    ):
        second.wait_recv()
        for k in range(3):
            own += landing[k].astype(F32)
        out[0] = own.astype(BF16)

    for group in groups:
        group.wait_send()
    for copy in put:
        copy.wait()


def hand_on(*refs):
    sources, targets, through, (get_sem, put_sem) = refs[:5], refs[5:10], refs[10:15], refs[15:]
    parts = []
    for n in range(5):
        for i in range(PARTS if n < 2 else 1):
            rows = pl.ds(i * (FEAT // PARTS), FEAT // PARTS) if n < 2 else 0
            parts.append([ref.at[rows] for ref in (sources[n], through[n], targets[n])])
    gets = [
        pltpu.make_async_copy(part[0], part[1], get_sem.at[i]) for i, part in enumerate(parts)
    ]
    puts = [
        pltpu.make_async_copy(part[1], part[2], put_sem.at[i]) for i, part in enumerate(parts)
    ]
    for get in gets:
        get.start()
    for get, put in zip(gets, puts):
        get.wait()
        put.start()
    for put in puts:
        put.wait()


def on_device(
    ffn_input,
    gate_act,
    up_act,
    hidden_grad,
    stream_grad,
    w_gate,
    w_up,
    gate_keep,
    up_keep,
    w_out,
    queries,
    keys,
    values,
):
    hbm = pl.BlockSpec(memory_space=pl.ANY)
    vmem = pl.BlockSpec(memory_space=pltpu.VMEM)
    smem = pl.BlockSpec(memory_space=pltpu.SMEM)
    chunk_grid = (4, 4, ROWS)
    out_shape = (
        jax.ShapeDtypeStruct((FEAT, HID), BF16),
        jax.ShapeDtypeStruct((FEAT, HID), BF16),
        jax.ShapeDtypeStruct((1, ROWS, HEADS * HD), BF16),
        jax.ShapeDtypeStruct((1, ROWS, HD), BF16),
        jax.ShapeDtypeStruct((1, ROWS, HD), BF16),
    )
    results = pl.pallas_call(
        kernel,
        out_shape=out_shape,
        in_specs=[hbm, vmem, vmem, vmem, hbm, hbm, hbm, smem, smem, hbm, hbm, vmem, vmem],
        out_specs=(hbm, hbm, vmem, vmem, vmem),
        scratch_shapes=[
            pltpu.VMEM(chunk_grid + (HID,), BF16),
            pltpu.VMEM(chunk_grid + (HID,), BF16),
            pltpu.VMEM(chunk_grid + (HD,), BF16),
            pltpu.VMEM(chunk_grid + (HD,), BF16),
            pltpu.VMEM((2, FEAT, HID), BF16),
            pltpu.VMEM((SEQ, FEAT), BF16),
            pltpu.VMEM((FEAT, SEQ), BF16),
            pltpu.VMEM((HEADS * HD, FEAT), BF16),
            pltpu.VMEM((ROWS, HEADS * HD), BF16),
            pltpu.VMEM((QS, HD), BF16),
            pltpu.VMEM((4, ROWS, HD), BF16),
            pltpu.VMEM((4, 8, ROWS, HD), BF16),
            pltpu.VMEM((4, 7, ROWS, HD), BF16),
            pltpu.VMEM((4, 4, 2, ROWS, HD), BF16),
            pltpu.VMEM(chunk_grid + (HEADS * HD,), BF16),
            pltpu.VMEM((3, 4, ROWS, 512), BF16),
            pltpu.VMEM((3, 4, ROWS, 512), BF16),
            pltpu.VMEM((3, ROWS, 512), BF16),
            pltpu.VMEM((3, ROWS, 512), BF16),
            pltpu.VMEM((3, ROWS, 512), BF16),
            pltpu.VMEM((3, ROWS, 512), BF16),
            pltpu.VMEM((ROWS, HEADS * HD), F32),
            pltpu.VMEM((QS, HD), BF16),
            pltpu.VMEM((2, FEAT, HID), BF16),
            pltpu.VMEM((2, FEAT, HID), BF16),
            pltpu.VMEM((2, FEAT, HID), BF16),
            pltpu.VMEM((HD, SEQ), BF16),
            pltpu.VMEM((HD, SEQ), BF16),
            pltpu.VMEM((HD, QS), F32),
            pltpu.VMEM((SEQ, QS), F32),
            pltpu.VMEM((SEQ, QS), BF16),
            pltpu.VMEM((SEQ, QS), BF16),
            pltpu.VMEM(chunk_grid + (HD,), BF16),
            pltpu.VMEM(chunk_grid + (HD,), BF16),
            pltpu.VMEM((3, 4, ROWS, HD), BF16),
            pltpu.VMEM((3, 4, ROWS, HD), BF16),
            pltpu.VMEM((3, ROWS, HD), BF16),
            pltpu.VMEM((3, ROWS, HD), BF16),
            pltpu.VMEM((3, ROWS, HD), BF16),
            pltpu.VMEM((3, ROWS, HD), BF16),
            pltpu.SemaphoreType.DMA((N_GROUPS,)),
            pltpu.SemaphoreType.DMA((N_GROUPS,)),
            pltpu.SemaphoreType.DMA((11,)),
        ],
        compiler_params=pltpu.CompilerParams(
            collective_id=0, has_side_effects=True, vmem_limit_bytes=56 * 1024 * 1024
        ),
    )(
        ffn_input,
        gate_act,
        up_act,
        hidden_grad,
        stream_grad.reshape(16, ROWS, FEAT),
        w_gate,
        w_up,
        gate_keep,
        up_keep,
        w_out,
        queries,
        keys,
        values,
    )
    return pl.pallas_call(
        hand_on,
        out_shape=out_shape,
        in_specs=[hbm] * 5,
        out_specs=(hbm,) * 5,
        scratch_shapes=[pltpu.VMEM(shape.shape, BF16) for shape in out_shape]
        + [pltpu.SemaphoreType.DMA((2 * PARTS + 3,))] * 2,
        compiler_params=pltpu.CompilerParams(vmem_limit_bytes=60 * 1024 * 1024),
    )(*results)


def solution(mesh):
    placed = (
        P("dp", None, "row"),
        P("dp", "row", "col"),
        P("dp", "row", "col"),
        P("dp", "row", "col"),
        P("dp", None, "row"),
        P("row", "col"),
        P("row", "col"),
        P("row", "col"),
        P("row", "col"),
        P("col", "row"),
        P("dp", "row", "col"),
        P("dp", "row", "col"),
        P("dp", "row", "col"),
    )
    return jax.shard_map(
        on_device,
        mesh=mesh,
        in_specs=placed,
        out_specs=(
            P("row", "col"),
            P("row", "col"),
            P("dp", "row", "col"),
            P("dp", "row", "col"),
            P("dp", "row", "col"),
        ),
        check_vma=False,
    )
```

```python
import math

import jax
import jax.numpy as jnp
from jax import lax
from jax.experimental import pallas as pl
from jax.experimental.pallas import tpu as pltpu
from jax.sharding import PartitionSpec as P

MESH = pl.DeviceIdType.MESH
F32 = jnp.float32
BF16 = jnp.bfloat16

ROWS = 80
PARTS = 4
HID = 1792
HALF = 896
FEAT = 256
SEQ = 1280
HEADS = 8
HD = 128
QS = HEADS * ROWS
SCALE = 1.0 / math.sqrt(HD)
NEGATIVE_FILL = -1e30
N_GROUPS = 46
OFFSETS = (-1, 1, 2)

QUARTERS = (
    ((0, 0), (0, -1), (-1, 0), (-1, -1)),
    ((0, 1), (1, 0), (-1, 1), (1, -1)),
    ((0, 2), (2, 0), (1, 2), (2, 1)),
    ((1, 1), (-1, 2), (2, -1), (2, 2)),
)

def pick(table, j):
    total = 0
    for k, value in enumerate(table):
        total = total + value * (1 - lax.div(lax.rem(j + (4 - k), 4) + 3, 4))
    return total


def nt(left, right):
    return lax.dot_general(left, right, (((1,), (1,)), ((), ())), preferred_element_type=F32)


def nn(left, right):
    return lax.dot_general(left, right, (((1,), (0,)), ((), ())), preferred_element_type=F32)


def kernel(
    ffn_hbm,
    gate_ref,
    up_ref,
    hidden_ref,
    stream_hbm,
    wg_hbm,
    wu_hbm,
    gk_ref,
    uk_ref,
    wo_hbm,
    q_hbm,
    k_ref,
    v_ref,
    gw_hbm,
    uw_hbm,
    dq_ref,
    dk_ref,
    dv_ref,
    ga,
    ua,
    k_all,
    v_all,
    w_eff,
    ffn_v,
    ffn_t,
    wout_v,
    q_v,
    q_s,
    stream_v,
    zs,
    zr,
    strm,
    hp,
    ra,
    rb,
    ha,
    hb,
    ra2,
    rb2,
    g_own,
    g_s,
    w_send,
    w_recv,
    w_out_v,
    k_t,
    v_t,
    out_t,
    p_f,
    p_low,
    ds_s,
    kt_s,
    vt_s,
    kt_r,
    vt_r,
    kt2_s,
    vt2_s,
    kt2_r,
    vt2_r,
    send_sem,
    recv_sem,
    local_sem,
):
    row = lax.axis_index("row")
    z = lax.axis_index("col")
    core = lax.axis_index("dp")
    y, x = row // 4, row % 4

    def ring(v, off):
        return lax.rem(v + (off + 4), 4)

    def dev(axis, off):
        if axis == "x":
            return {"row": y * 4 + ring(x, off)}
        return {"row": ring(y, off) * 4 + x}

    groups = []

    class Group:
        def __init__(self, size):
            self.i, self.size = len(groups), size
            groups.append(self)

        def copy(self, src, dst, device):
            return pltpu.make_async_remote_copy(
                src_ref=src,
                dst_ref=dst,
                send_sem=send_sem.at[self.i],
                recv_sem=recv_sem.at[self.i],
                device_id=device,
                device_id_type=MESH,
            )

        def send(self, src, dst, device):
            self.copy(src, dst, device).start()

        def wait_recv(self):
            self.copy(self.size, self.size, {"dp": 1 - core}).wait_recv()

        def wait_send(self):
            self.copy(self.size, self.size, {"dp": 1 - core}).wait_send()

    barrier = pltpu.get_barrier_semaphore()
    partners = [dev("x", o) for o in OFFSETS] + [dev("y", o) for o in OFFSETS]
    partners += [{"col": lax.rem(z + o, 8)} for o in range(1, 8)] + [{"dp": 1 - core}]
    for partner in partners:
        pl.semaphore_signal(barrier, inc=1, device_id=partner, device_id_type=MESH)

    def fetch(i, src, dst):
        copy = pltpu.make_async_copy(src, dst, local_sem.at[i])
        copy.start()
        return copy

    def place(chunk):
        dy, dx = chunk
        return lax.rem(y + dy + 4, 4), lax.rem(x + dx + 4, 4)

    mine = []
    for quarter in QUARTERS:
        mine.append(place([pick([chunk[i] for chunk in quarter], z // 2) for i in range(2)]))
    side = lax.rem(z, 2)
    side_cols = pl.ds(pl.multiple_of(side * HD, HD), HD)
    get_wg = fetch(0, wg_hbm, w_eff.at[0])
    get_wu = fetch(1, wu_hbm, w_eff.at[1])
    get_ffn = fetch(2, ffn_hbm.at[0], ffn_v)
    get_wo = fetch(3, wo_hbm, wout_v)
    get_q = fetch(4, q_hbm.at[0], q_v)
    get_st = [
        fetch(5 + b, stream_hbm.at[mine[b][0] * 4 + mine[b][1], :, side_cols], stream_v.at[b])
        for b in range(4)
    ]

    def act_step(i, _):
        cols = pl.ds(pl.multiple_of(i * 128, 128), 128)
        gate_f = gate_ref[0, :, cols].astype(F32)
        hidden_f = hidden_ref[0, :, cols].astype(F32)
        sigma = jax.nn.sigmoid(gate_f)
        ua[y, x, :, cols] = (hidden_f * gate_f * sigma).astype(BF16)
        ga[y, x, :, cols] = (
            hidden_f * up_ref[0, :, cols].astype(F32) * sigma * (1.0 + gate_f * (1.0 - sigma))
        ).astype(BF16)
        return 0

    lax.fori_loop(0, HID // 128, act_step, 0, unroll=7)
    k_all[y, x] = k_ref[0]
    v_all[y, x] = v_ref[0]

    pl.semaphore_wait(barrier, len(partners))

    arrays = ((ga, "x", "y"), (ua, "y", "x"))

    def at(n, first, second):
        arr, p, _ = arrays[n]
        if p == "x":
            return arr.at[ring(y, second), ring(x, first)]
        return arr.at[ring(y, first), ring(x, second)]

    two_chunks = ga.at[0, 0:2]
    along = {(n, d): Group(at(n, 0, 0)) for n in range(2) for d in (1, -1)}
    relay = [Group(at(n, 2, 0)) for n in range(2)]
    across = {(n, first): Group(two_chunks) for n in range(2) for first in (0, -1, 1, 2)}
    far = {(n, part): Group(two_chunks) for n in range(2) for part in range(2)}

    def spread(n, first):
        block = at(n, first, 0)
        for d in (1, -1):
            across[n, first].send(block, block, dev(arrays[n][2], d))

    for n in range(2):
        for d in (1, -1):
            along[n, d].send(at(n, 0, 0), at(n, 0, 0), dev(arrays[n][1], d))
    for n in range(2):
        spread(n, 0)

    keys1, values1 = Group(k_all.at[0, 0:3]), Group(v_all.at[0, 0:3])
    keys2, values2 = Group(k_all.at[0:3]), Group(v_all.at[0:3])

    for n, (get, keep) in enumerate(((get_wg, gk_ref), (get_wu, uk_ref))):
        get.wait()

        def mask_step(j, _, n=n, keep=keep):
            cols = pl.ds(pl.multiple_of(j * 128, 128), 128)
            for i in range(2):
                rows = slice(i * 128, (i + 1) * 128)
                tile = w_eff[n, rows, cols].astype(F32) * keep[i, j].astype(F32)
                w_eff[n, rows, cols] = tile.astype(BF16)
            return 0

        lax.fori_loop(0, HID // 128, mask_step, 0)

    for d in (1, -1):
        for n in range(2):
            along[n, d].wait_recv()
            cols = slice(0, HALF) if d == 1 else slice(HALF, HID)
            part = at(n, -d, 0).at[:, cols]
            relay[n].send(part, part, dev(arrays[n][1], d))
            spread(n, -d)

    get_ffn.wait()

    def transpose_step(i, _):
        rows = pl.ds(pl.multiple_of(i * 256, 256), 256)
        ffn_t[:, rows] = ffn_v[rows, :].T
        return 0

    lax.fori_loop(0, SEQ // 256, transpose_step, 0)
    get_q.wait()
    for h in range(HEADS):
        q_s[h * ROWS : (h + 1) * ROWS, :] = q_v[:, h * HD : (h + 1) * HD]

    for n in range(2):
        relay[n].wait_recv()
        spread(n, 2)

    col_sum = [Group(zr.at[b]) for b in range(4)]
    col_all = [Group(zr.at[b]) for b in range(4)]

    def terms(n, chunks):
        spots = [place(c) for c in chunks]
        rows = jnp.concatenate([arrays[n][0][yc, xc, :, :] for yc, xc in spots], axis=0)
        return nt(rows, w_eff[n])

    def send_sums(b, i, total):
        for j in range(2):
            zs[b, i * 2 + j] = total[:, j * HD : (j + 1) * HD].astype(BF16)

    def scatter_col(b):
        for off in range(1, 8):
            to = lax.rem(z + off, 8)
            col_sum[b].send(zs.at[b, to], zr.at[b, off - 1], {"col": to})

    def input_terms(b):
        total = terms(0, QUARTERS[b]) + terms(1, QUARTERS[b])
        for i in range(4):
            send_sums(b, i, total[i * ROWS : (i + 1) * ROWS])
        scatter_col(b)

    def gather_col(b):
        col_sum[b].wait_recv()
        get_st[b].wait()
        total = zs[b, z].astype(F32)
        for j in range(7):
            total += zr[b, j].astype(F32)
        yc, xc = mine[b]
        strm[yc, xc, side] = (stream_v[b].astype(F32) + total).astype(BF16)
        block = strm.at[yc, xc, side]
        for off in range(1, 8):
            col_all[b].send(block, block, {"col": lax.rem(z + off, 8)})

    first_a = {dy: Group(ra2) for dy in (0, -1, 1, 2)}
    first_b = {dx: Group(rb2) for dx in (0, -1, 1, 2)}

    def head_terms(b, at_once=True):
        col_all[b].wait_recv()
        spots = [place(c) for c in QUARTERS[b]]
        total = jnp.concatenate(
            [
                jnp.concatenate([strm[yc, xc, j] for yc, xc in spots], axis=0) for j in range(2)
            ],
            axis=1,
        )

        def step(t, _):
            cols = pl.ds(pl.multiple_of(t * 256, 256), 256)
            part = nt(total, wout_v[cols, :]).astype(BF16)
            for i, (yc, xc) in enumerate(spots):
                hp[yc, xc, :, cols] = part[i * ROWS : (i + 1) * ROWS, :]
            return 0

        lax.fori_loop(0, 2, step, 0)
        if at_once:
            send_a(b)
        lax.fori_loop(2, 4, step, 0)
        if at_once:
            send_b(b)

    def send_a(b):
        for dy, dx in QUARTERS[b][::-1]:
            yc, xc = place((dy, dx))
            if dx != 0:
                first_a[dy].send(
                    hp.at[yc, xc, :, 0:512], ra.at[OFFSETS.index(dx), yc], dev("x", dx)
                )

    def send_b(b):
        for dy, dx in QUARTERS[b][::-1]:
            yc, xc = place((dy, dx))
            if dy != 0:
                first_b[dx].send(
                    hp.at[yc, xc, :, 512:1024], rb.at[OFFSETS.index(dy), xc], dev("y", dy)
                )

    for first, d, part in ((0, 1, 0), (-1, 1, 1), (1, -1, 0), (2, -1, 1)):
        for n in range(2):
            across[n, first].wait_recv()
            block = at(n, first, -d)
            far[n, part].send(block, block, dev(arrays[n][2], d))
        if first == -1:
            input_terms(0)
        if first == 1:
            input_terms(1)

    for o in OFFSETS:
        keys1.send(k_all.at[y, x], k_all.at[y, x], dev("x", o))
        values1.send(v_all.at[y, x], v_all.at[y, x], dev("y", o))

    gather_col(0)
    gather_col(1)
    get_wo.wait()
    head_terms(0, at_once=False)
    for n in range(2):
        far[n, 0].wait_recv()
    input_terms(2)
    for n in range(2):
        far[n, 1].wait_recv()
    input_terms(3)
    keys1.wait_recv()
    values1.wait_recv()
    for o in OFFSETS:
        keys2.send(k_all.at[y], k_all.at[y], dev("y", o))
        values2.send(v_all.at[:, x], v_all.at[:, x], dev("x", o))
    send_a(0)
    send_b(0)

    def wgrad(n):
        arr = arrays[n][0]

        def step(t, _):
            cols = pl.ds(pl.multiple_of(t * 256, 256), 256)
            tokens = arr[:, :, :, cols].reshape(SEQ, 256)
            w_send[n, :, cols] = nn(ffn_t[...], tokens).astype(BF16)
            return 0

        lax.fori_loop(0, HID // 256, step, 0)
        pair[n].send(w_send.at[n], w_recv.at[n], {"dp": 1 - core})

    pair = [Group(w_recv.at[n]) for n in range(2)]
    head_terms(1)
    gather_col(2)
    wgrad(0)
    gather_col(3)
    head_terms(2)
    head_terms(3)
    wgrad(1)

    keys2.wait_recv()
    values2.wait_recv()
    k_t[...] = k_all[...].reshape(SEQ, HD).T
    v_t[...] = v_all[...].reshape(SEQ, HD).T

    def softmax_step(t, _):
        cols = pl.ds(pl.multiple_of(t * 128, 128), 128)
        scores = nt(k_all[...].reshape(SEQ, HD), q_s[cols, :]) * SCALE
        lane = lax.broadcasted_iota(jnp.int32, (1, 128), 1) + t * 128
        head = jnp.zeros_like(lane)
        for h in range(1, HEADS):
            head += (lane >= h * ROWS).astype(jnp.int32)
        query_pos = lane - head * ROWS + row * ROWS
        key_pos = lax.broadcasted_iota(jnp.int32, (SEQ, 128), 0)
        scores = jnp.where(key_pos <= query_pos, scores, NEGATIVE_FILL)
        weight = jnp.exp(scores - jnp.max(scores, axis=0, keepdims=True))
        probs = weight * (1.0 / jnp.sum(weight, axis=0, keepdims=True))
        p_f[:, cols] = probs
        p_low[:, cols] = probs.astype(BF16)
        out_t[:, cols] = nn(v_t[...], p_low[:, cols])
        return 0

    lax.fori_loop(0, QS // 128, softmax_step, 0)

    second_a, second_b = Group(ra2), Group(rb2)
    for off in (2, -1, 1, 0):
        first_a[off].wait_recv()
        first_b[off].wait_recv()
        yc, xc = ring(y, off), ring(x, off)
        total_a = hp[yc, x, :, 0:512].astype(F32)
        total_b = hp[y, xc, :, 512:1024].astype(F32)
        for k in range(3):
            total_a += ra[k, yc].astype(F32)
            total_b += rb[k, xc].astype(F32)
        if off == 0:
            g_own[:, 0:512] = total_a
            g_own[:, 512:1024] = total_b
        else:
            k = OFFSETS.index(off)
            ha[k] = total_a.astype(BF16)
            hb[k] = total_b.astype(BF16)
            second_a.send(ha.at[k], ra2.at[k], dev("y", off))
            second_b.send(hb.at[k], rb2.at[k], dev("x", off))

    put = []
    for n, (keep, out) in enumerate(((gk_ref, gw_hbm), (uk_ref, uw_hbm))):
        pair[n].wait_recv()

        def sum_step(j, _, n=n, keep=keep):
            cols = pl.ds(pl.multiple_of(j * 128, 128), 128)
            for i in range(2):
                rows = slice(i * 128, (i + 1) * 128)
                total = w_send[n, rows, cols].astype(F32) + w_recv[n, rows, cols].astype(F32)
                w_out_v[n, rows, cols] = (total * keep[i, j].astype(F32)).astype(BF16)
            return 0

        lax.fori_loop(0, HID // 128, sum_step, 0)
        put.append(fetch(9 + n, w_out_v.at[n], out))

    second_a.wait_recv()
    second_b.wait_recv()
    for h in range(HEADS):
        cols = slice(h * HD, (h + 1) * HD)
        total = g_own[:, cols]
        buf = ra2 if h < 4 else rb2
        low = slice((h % 4) * HD, (h % 4 + 1) * HD)
        for k in range(3):
            total += buf[k, :, low].astype(F32)
        g_s[h * ROWS : (h + 1) * ROWS, :] = total.astype(BF16)

    val1, val2 = Group(vt_r), Group(vt2_r)
    key1, key2 = Group(kt_r), Group(kt2_r)
    delta = jnp.sum(out_t[...] * g_s[...].astype(F32).T, axis=0, keepdims=True)
    for off in (2, -1, 1, 0):
        yc = ring(y, off)
        rows = pl.ds(pl.multiple_of(yc * 320, 320), 320)
        prob_grad = nt(v_all[yc].reshape(320, HD), g_s[...])
        part = nn(p_low[rows, :], g_s[...]).astype(BF16)
        for i in range(4):
            vt_s[yc, i] = part[i * ROWS : (i + 1) * ROWS, :]
        if off != 0:
            val1.send(vt_s.at[yc], vt_r.at[OFFSETS.index(off)], dev("y", off))
        score = (p_f[rows, :] * (prob_grad - delta) * SCALE).astype(BF16)
        ds_s[rows, :] = score
        part = nn(score, q_s[...]).astype(BF16)
        for i in range(4):
            kt_s[yc, i] = part[i * ROWS : (i + 1) * ROWS, :]
        for k, o in enumerate(OFFSETS):
            xc = ring(x, o)
            key1.send(kt_s.at[yc, xc], kt_r.at[k, yc], dev("x", o))

    def q_step(t, _):
        cols = pl.ds(pl.multiple_of(t * 128, 128), 128)
        q_s[cols, :] = nn(k_t[...], ds_s[:, cols]).T.astype(BF16)
        return 0

    lax.fori_loop(0, QS // 128, q_step, 0)
    for h in range(HEADS):
        dq_ref[0, :, h * HD : (h + 1) * HD] = q_s[h * ROWS : (h + 1) * ROWS, :]

    def add_up(first, own, recv, buf, axis, keep_at, second, landing):
        first.wait_recv()
        for k, o in enumerate(OFFSETS):
            spot = ring(keep_at, o)
            total = own(spot).astype(F32)
            for j in range(3):
                total += recv[j, spot].astype(F32)
            buf[k] = total.astype(BF16)
            second.send(buf.at[k], landing.at[k], dev(axis, o))
        total = own(keep_at).astype(F32)
        for j in range(3):
            total += recv[j, keep_at].astype(F32)
        return total

    val_own = add_up(val1, lambda i: vt_s[y, i], vt_r, vt2_s, "x", x, val2, vt2_r)
    key_own = add_up(key1, lambda i: kt_s[i, x], kt_r, kt2_s, "y", y, key2, kt2_r)
    for own, second, landing, out in (
        (val_own, val2, vt2_r, dv_ref),
        (key_own, key2, kt2_r, dk_ref),
    ):
        second.wait_recv()
        for k in range(3):
            own += landing[k].astype(F32)
        out[0] = own.astype(BF16)

    for group in groups:
        group.wait_send()
    for copy in put:
        copy.wait()


def hand_on(*refs):
    sources, targets, through, (get_sem, put_sem) = refs[:5], refs[5:10], refs[10:15], refs[15:]
    parts = []
    for n in range(5):
        for i in range(PARTS if n < 2 else 1):
            rows = pl.ds(i * (FEAT // PARTS), FEAT // PARTS) if n < 2 else 0
            parts.append([ref.at[rows] for ref in (sources[n], through[n], targets[n])])
    gets = [
        pltpu.make_async_copy(part[0], part[1], get_sem.at[i]) for i, part in enumerate(parts)
    ]
    puts = [
        pltpu.make_async_copy(part[1], part[2], put_sem.at[i]) for i, part in enumerate(parts)
    ]
    for get in gets:
        get.start()
    for get, put in zip(gets, puts):
        get.wait()
        put.start()
    for put in puts:
        put.wait()


def on_device(
    ffn_input,
    gate_act,
    up_act,
    hidden_grad,
    stream_grad,
    w_gate,
    w_up,
    gate_keep,
    up_keep,
    w_out,
    queries,
    keys,
    values,
):
    hbm = pl.BlockSpec(memory_space=pl.ANY)
    vmem = pl.BlockSpec(memory_space=pltpu.VMEM)
    smem = pl.BlockSpec(memory_space=pltpu.SMEM)
    chunk_grid = (4, 4, ROWS)
    out_shape = (
        jax.ShapeDtypeStruct((FEAT, HID), BF16),
        jax.ShapeDtypeStruct((FEAT, HID), BF16),
        jax.ShapeDtypeStruct((1, ROWS, HEADS * HD), BF16),
        jax.ShapeDtypeStruct((1, ROWS, HD), BF16),
        jax.ShapeDtypeStruct((1, ROWS, HD), BF16),
    )
    results = pl.pallas_call(
        kernel,
        out_shape=out_shape,
        in_specs=[hbm, vmem, vmem, vmem, hbm, hbm, hbm, smem, smem, hbm, hbm, vmem, vmem],
        out_specs=(hbm, hbm, vmem, vmem, vmem),
        scratch_shapes=[
            pltpu.VMEM(chunk_grid + (HID,), BF16),
            pltpu.VMEM(chunk_grid + (HID,), BF16),
            pltpu.VMEM(chunk_grid + (HD,), BF16),
            pltpu.VMEM(chunk_grid + (HD,), BF16),
            pltpu.VMEM((2, FEAT, HID), BF16),
            pltpu.VMEM((SEQ, FEAT), BF16),
            pltpu.VMEM((FEAT, SEQ), BF16),
            pltpu.VMEM((HEADS * HD, FEAT), BF16),
            pltpu.VMEM((ROWS, HEADS * HD), BF16),
            pltpu.VMEM((QS, HD), BF16),
            pltpu.VMEM((4, ROWS, HD), BF16),
            pltpu.VMEM((4, 8, ROWS, HD), BF16),
            pltpu.VMEM((4, 7, ROWS, HD), BF16),
            pltpu.VMEM((4, 4, 2, ROWS, HD), BF16),
            pltpu.VMEM(chunk_grid + (HEADS * HD,), BF16),
            pltpu.VMEM((3, 4, ROWS, 512), BF16),
            pltpu.VMEM((3, 4, ROWS, 512), BF16),
            pltpu.VMEM((3, ROWS, 512), BF16),
            pltpu.VMEM((3, ROWS, 512), BF16),
            pltpu.VMEM((3, ROWS, 512), BF16),
            pltpu.VMEM((3, ROWS, 512), BF16),
            pltpu.VMEM((ROWS, HEADS * HD), F32),
            pltpu.VMEM((QS, HD), BF16),
            pltpu.VMEM((2, FEAT, HID), BF16),
            pltpu.VMEM((2, FEAT, HID), BF16),
            pltpu.VMEM((2, FEAT, HID), BF16),
            pltpu.VMEM((HD, SEQ), BF16),
            pltpu.VMEM((HD, SEQ), BF16),
            pltpu.VMEM((HD, QS), F32),
            pltpu.VMEM((SEQ, QS), F32),
            pltpu.VMEM((SEQ, QS), BF16),
            pltpu.VMEM((SEQ, QS), BF16),
            pltpu.VMEM(chunk_grid + (HD,), BF16),
            pltpu.VMEM(chunk_grid + (HD,), BF16),
            pltpu.VMEM((3, 4, ROWS, HD), BF16),
            pltpu.VMEM((3, 4, ROWS, HD), BF16),
            pltpu.VMEM((3, ROWS, HD), BF16),
            pltpu.VMEM((3, ROWS, HD), BF16),
            pltpu.VMEM((3, ROWS, HD), BF16),
            pltpu.VMEM((3, ROWS, HD), BF16),
            pltpu.SemaphoreType.DMA((N_GROUPS,)),
            pltpu.SemaphoreType.DMA((N_GROUPS,)),
            pltpu.SemaphoreType.DMA((11,)),
        ],
        compiler_params=pltpu.CompilerParams(
            collective_id=0, has_side_effects=True, vmem_limit_bytes=56 * 1024 * 1024
        ),
    )(
        ffn_input,
        gate_act,
        up_act,
        hidden_grad,
        stream_grad.reshape(16, ROWS, FEAT),
        w_gate,
        w_up,
        gate_keep,
        up_keep,
        w_out,
        queries,
        keys,
        values,
    )
    return pl.pallas_call(
        hand_on,
        out_shape=out_shape,
        in_specs=[hbm] * 5,
        out_specs=(hbm,) * 5,
        scratch_shapes=[pltpu.VMEM(shape.shape, BF16) for shape in out_shape]
        + [pltpu.SemaphoreType.DMA((2 * PARTS + 3,))] * 2,
        compiler_params=pltpu.CompilerParams(vmem_limit_bytes=60 * 1024 * 1024),
    )(*results)


def solution(mesh):
    placed = (
        P("dp", None, "row"),
        P("dp", "row", "col"),
        P("dp", "row", "col"),
        P("dp", "row", "col"),
        P("dp", None, "row"),
        P("row", "col"),
        P("row", "col"),
        P("row", "col"),
        P("row", "col"),
        P("col", "row"),
        P("dp", "row", "col"),
        P("dp", "row", "col"),
        P("dp", "row", "col"),
    )
    return jax.shard_map(
        on_device,
        mesh=mesh,
        in_specs=placed,
        out_specs=(
            P("row", "col"),
            P("row", "col"),
            P("dp", "row", "col"),
            P("dp", "row", "col"),
            P("dp", "row", "col"),
        ),
        check_vma=False,
    )
```

```python
import math

import jax
import jax.numpy as jnp
from jax import lax
from jax.experimental import pallas as pl
from jax.experimental.pallas import tpu as pltpu
from jax.sharding import PartitionSpec as P

MESH = pl.DeviceIdType.MESH
F32 = jnp.float32
BF16 = jnp.bfloat16

ROWS = 80
PARTS = 4
HID = 1792
HALF = 896
FEAT = 256
SEQ = 1280
HEADS = 8
HD = 128
QS = HEADS * ROWS
SCALE = 1.0 / math.sqrt(HD)
NEGATIVE_FILL = -1e30
N_GROUPS = 46
OFFSETS = (-1, 1, 2)

QUARTERS = (
    ((0, 0), (0, -1), (-1, 0), (0, 1)),
    ((1, 0), (-1, -1), (-1, 1), (1, -1)),
    ((0, 2), (2, 0), (1, 2), (2, 1)),
    ((1, 1), (-1, 2), (2, -1), (2, 2)),
)

def pick(table, j):
    total = 0
    for k, value in enumerate(table):
        total = total + value * (1 - lax.div(lax.rem(j + (4 - k), 4) + 3, 4))
    return total


def nt(left, right):
    return lax.dot_general(left, right, (((1,), (1,)), ((), ())), preferred_element_type=F32)


def nn(left, right):
    return lax.dot_general(left, right, (((1,), (0,)), ((), ())), preferred_element_type=F32)


def kernel(
    ffn_hbm,
    gate_ref,
    up_ref,
    hidden_ref,
    stream_hbm,
    wg_hbm,
    wu_hbm,
    gk_ref,
    uk_ref,
    wo_hbm,
    q_hbm,
    k_ref,
    v_ref,
    gw_hbm,
    uw_hbm,
    dq_ref,
    dk_ref,
    dv_ref,
    ga,
    ua,
    k_all,
    v_all,
    w_eff,
    ffn_v,
    ffn_t,
    wout_v,
    q_v,
    q_s,
    stream_v,
    zs,
    zr,
    strm,
    hp,
    ra,
    rb,
    ha,
    hb,
    ra2,
    rb2,
    g_own,
    g_s,
    w_send,
    w_recv,
    w_out_v,
    k_t,
    v_t,
    out_t,
    p_f,
    p_low,
    ds_s,
    kt_s,
    vt_s,
    kt_r,
    vt_r,
    kt2_s,
    vt2_s,
    kt2_r,
    vt2_r,
    send_sem,
    recv_sem,
    local_sem,
):
    row = lax.axis_index("row")
    z = lax.axis_index("col")
    core = lax.axis_index("dp")
    y, x = row // 4, row % 4

    def ring(v, off):
        return lax.rem(v + (off + 4), 4)

    def dev(axis, off):
        if axis == "x":
            return {"row": y * 4 + ring(x, off)}
        return {"row": ring(y, off) * 4 + x}

    groups = []

    class Group:
        def __init__(self, size):
            self.i, self.size = len(groups), size
            groups.append(self)

        def copy(self, src, dst, device):
            return pltpu.make_async_remote_copy(
                src_ref=src,
                dst_ref=dst,
                send_sem=send_sem.at[self.i],
                recv_sem=recv_sem.at[self.i],
                device_id=device,
                device_id_type=MESH,
            )

        def send(self, src, dst, device):
            self.copy(src, dst, device).start()

        def wait_recv(self):
            self.copy(self.size, self.size, {"dp": 1 - core}).wait_recv()

        def wait_send(self):
            self.copy(self.size, self.size, {"dp": 1 - core}).wait_send()

    barrier = pltpu.get_barrier_semaphore()
    partners = [dev("x", o) for o in OFFSETS] + [dev("y", o) for o in OFFSETS]
    partners += [{"col": lax.rem(z + o, 8)} for o in range(1, 8)] + [{"dp": 1 - core}]
    for partner in partners:
        pl.semaphore_signal(barrier, inc=1, device_id=partner, device_id_type=MESH)

    def fetch(i, src, dst):
        copy = pltpu.make_async_copy(src, dst, local_sem.at[i])
        copy.start()
        return copy

    def place(chunk):
        dy, dx = chunk
        return lax.rem(y + dy + 4, 4), lax.rem(x + dx + 4, 4)

    mine = []
    for quarter in QUARTERS:
        mine.append(place([pick([chunk[i] for chunk in quarter], z // 2) for i in range(2)]))
    side = lax.rem(z, 2)
    side_cols = pl.ds(pl.multiple_of(side * HD, HD), HD)
    get_wg = fetch(0, wg_hbm, w_eff.at[0])
    get_wu = fetch(1, wu_hbm, w_eff.at[1])
    get_ffn = fetch(2, ffn_hbm.at[0], ffn_v)
    get_wo = fetch(3, wo_hbm, wout_v)
    get_q = fetch(4, q_hbm.at[0], q_v)
    get_st = [
        fetch(5 + b, stream_hbm.at[mine[b][0] * 4 + mine[b][1], :, side_cols], stream_v.at[b])
        for b in range(4)
    ]

    def act_step(i, _):
        cols = pl.ds(pl.multiple_of(i * 128, 128), 128)
        gate_f = gate_ref[0, :, cols].astype(F32)
        hidden_f = hidden_ref[0, :, cols].astype(F32)
        sigma = jax.nn.sigmoid(gate_f)
        ua[y, x, :, cols] = (hidden_f * gate_f * sigma).astype(BF16)
        ga[y, x, :, cols] = (
            hidden_f * up_ref[0, :, cols].astype(F32) * sigma * (1.0 + gate_f * (1.0 - sigma))
        ).astype(BF16)
        return 0

    lax.fori_loop(0, HID // 128, act_step, 0, unroll=7)
    k_all[y, x] = k_ref[0]
    v_all[y, x] = v_ref[0]

    pl.semaphore_wait(barrier, len(partners))

    arrays = ((ga, "x", "y"), (ua, "y", "x"))

    def at(n, first, second):
        arr, p, _ = arrays[n]
        if p == "x":
            return arr.at[ring(y, second), ring(x, first)]
        return arr.at[ring(y, first), ring(x, second)]

    two_chunks = ga.at[0, 0:2]
    along = {(n, d): Group(at(n, 0, 0)) for n in range(2) for d in (1, -1)}
    relay = [Group(at(n, 2, 0)) for n in range(2)]
    across = {(n, first): Group(two_chunks) for n in range(2) for first in (0, -1, 1, 2)}
    far = {(n, part): Group(two_chunks) for n in range(2) for part in range(2)}

    def spread(n, first):
        block = at(n, first, 0)
        for d in (1, -1):
            across[n, first].send(block, block, dev(arrays[n][2], d))

    for n in range(2):
        for d in (1, -1):
            along[n, d].send(at(n, 0, 0), at(n, 0, 0), dev(arrays[n][1], d))
    for n in range(2):
        spread(n, 0)

    keys1, values1 = Group(k_all.at[0, 0:3]), Group(v_all.at[0, 0:3])
    keys2, values2 = Group(k_all.at[0:3]), Group(v_all.at[0:3])

    for n, (get, keep) in enumerate(((get_wg, gk_ref), (get_wu, uk_ref))):
        get.wait()

        def mask_step(j, _, n=n, keep=keep):
            cols = pl.ds(pl.multiple_of(j * 128, 128), 128)
            for i in range(2):
                rows = slice(i * 128, (i + 1) * 128)
                tile = w_eff[n, rows, cols].astype(F32) * keep[i, j].astype(F32)
                w_eff[n, rows, cols] = tile.astype(BF16)
            return 0

        lax.fori_loop(0, HID // 128, mask_step, 0)

    for d in (1, -1):
        for n in range(2):
            along[n, d].wait_recv()
            cols = slice(0, HALF) if d == 1 else slice(HALF, HID)
            part = at(n, -d, 0).at[:, cols]
            relay[n].send(part, part, dev(arrays[n][1], d))
            spread(n, -d)

    get_ffn.wait()

    def transpose_step(i, _):
        rows = pl.ds(pl.multiple_of(i * 256, 256), 256)
        ffn_t[:, rows] = ffn_v[rows, :].T
        return 0

    lax.fori_loop(0, SEQ // 256, transpose_step, 0)
    get_q.wait()
    for h in range(HEADS):
        q_s[h * ROWS : (h + 1) * ROWS, :] = q_v[:, h * HD : (h + 1) * HD]

    for n in range(2):
        relay[n].wait_recv()
        spread(n, 2)

    col_sum = [Group(zr.at[b]) for b in range(4)]
    col_all = [Group(zr.at[b]) for b in range(4)]

    def terms(n, chunks):
        spots = [place(c) for c in chunks]
        rows = jnp.concatenate([arrays[n][0][yc, xc, :, :] for yc, xc in spots], axis=0)
        return nt(rows, w_eff[n])

    def send_sums(b, i, total):
        for j in range(2):
            zs[b, i * 2 + j] = total[:, j * HD : (j + 1) * HD].astype(BF16)

    def scatter_col(b):
        for off in range(1, 8):
            to = lax.rem(z + off, 8)
            col_sum[b].send(zs.at[b, to], zr.at[b, off - 1], {"col": to})

    def input_terms(b):
        total = terms(0, QUARTERS[b]) + terms(1, QUARTERS[b])
        for i in range(4):
            send_sums(b, i, total[i * ROWS : (i + 1) * ROWS])
        scatter_col(b)

    def gather_col(b):
        col_sum[b].wait_recv()
        get_st[b].wait()
        total = zs[b, z].astype(F32)
        for j in range(7):
            total += zr[b, j].astype(F32)
        yc, xc = mine[b]
        strm[yc, xc, side] = (stream_v[b].astype(F32) + total).astype(BF16)
        block = strm.at[yc, xc, side]
        for off in range(1, 8):
            col_all[b].send(block, block, {"col": lax.rem(z + off, 8)})

    first_a = {dy: Group(ra2) for dy in (0, -1, 1, 2)}
    first_b = {dx: Group(rb2) for dx in (0, -1, 1, 2)}

    def head_terms(b, at_once=True):
        col_all[b].wait_recv()
        spots = [place(c) for c in QUARTERS[b]]
        total = jnp.concatenate(
            [
                jnp.concatenate([strm[yc, xc, j] for yc, xc in spots], axis=0) for j in range(2)
            ],
            axis=1,
        )

        def step(t, _):
            cols = pl.ds(pl.multiple_of(t * 256, 256), 256)
            part = nt(total, wout_v[cols, :]).astype(BF16)
            for i, (yc, xc) in enumerate(spots):
                hp[yc, xc, :, cols] = part[i * ROWS : (i + 1) * ROWS, :]
            return 0

        lax.fori_loop(0, 2, step, 0)
        if at_once:
            send_a(b)
        lax.fori_loop(2, 4, step, 0)
        if at_once:
            send_b(b)

    def send_a(b):
        for dy, dx in QUARTERS[b][::-1]:
            yc, xc = place((dy, dx))
            if dx != 0:
                first_a[dy].send(
                    hp.at[yc, xc, :, 0:512], ra.at[OFFSETS.index(dx), yc], dev("x", dx)
                )

    def send_b(b):
        for dy, dx in QUARTERS[b][::-1]:
            yc, xc = place((dy, dx))
            if dy != 0:
                first_b[dx].send(
                    hp.at[yc, xc, :, 512:1024], rb.at[OFFSETS.index(dy), xc], dev("y", dy)
                )

    for first, d, part in ((0, 1, 0), (-1, 1, 1), (1, -1, 0), (2, -1, 1)):
        for n in range(2):
            across[n, first].wait_recv()
            block = at(n, first, -d)
            far[n, part].send(block, block, dev(arrays[n][2], d))
        if first == 0:
            input_terms(0)
        if first == 1:
            input_terms(1)

    for o in OFFSETS:
        keys1.send(k_all.at[y, x], k_all.at[y, x], dev("x", o))
        values1.send(v_all.at[y, x], v_all.at[y, x], dev("y", o))

    gather_col(0)
    gather_col(1)
    get_wo.wait()
    head_terms(0, at_once=False)
    for n in range(2):
        far[n, 0].wait_recv()
    input_terms(2)
    for n in range(2):
        far[n, 1].wait_recv()
    input_terms(3)
    keys1.wait_recv()
    values1.wait_recv()
    for o in OFFSETS:
        keys2.send(k_all.at[y], k_all.at[y], dev("y", o))
        values2.send(v_all.at[:, x], v_all.at[:, x], dev("x", o))
    send_a(0)
    send_b(0)

    def wgrad(n):
        arr = arrays[n][0]

        def step(t, _):
            cols = pl.ds(pl.multiple_of(t * 256, 256), 256)
            tokens = arr[:, :, :, cols].reshape(SEQ, 256)
            w_send[n, :, cols] = nn(ffn_t[...], tokens).astype(BF16)
            return 0

        lax.fori_loop(0, HID // 256, step, 0)
        pair[n].send(w_send.at[n], w_recv.at[n], {"dp": 1 - core})

    pair = [Group(w_recv.at[n]) for n in range(2)]
    head_terms(1)
    gather_col(2)
    wgrad(0)
    gather_col(3)
    head_terms(2)
    head_terms(3)
    wgrad(1)

    keys2.wait_recv()
    values2.wait_recv()
    k_t[...] = k_all[...].reshape(SEQ, HD).T
    v_t[...] = v_all[...].reshape(SEQ, HD).T

    def softmax_step(t, _):
        cols = pl.ds(pl.multiple_of(t * 128, 128), 128)
        scores = nt(k_all[...].reshape(SEQ, HD), q_s[cols, :]) * SCALE
        lane = lax.broadcasted_iota(jnp.int32, (1, 128), 1) + t * 128
        head = jnp.zeros_like(lane)
        for h in range(1, HEADS):
            head += (lane >= h * ROWS).astype(jnp.int32)
        query_pos = lane - head * ROWS + row * ROWS
        key_pos = lax.broadcasted_iota(jnp.int32, (SEQ, 128), 0)
        scores = jnp.where(key_pos <= query_pos, scores, NEGATIVE_FILL)
        weight = jnp.exp(scores - jnp.max(scores, axis=0, keepdims=True))
        probs = weight * (1.0 / jnp.sum(weight, axis=0, keepdims=True))
        p_f[:, cols] = probs
        p_low[:, cols] = probs.astype(BF16)
        out_t[:, cols] = nn(v_t[...], p_low[:, cols])
        return 0

    lax.fori_loop(0, QS // 128, softmax_step, 0)

    second_a, second_b = Group(ra2), Group(rb2)
    for off in (2, -1, 1, 0):
        first_a[off].wait_recv()
        first_b[off].wait_recv()
        yc, xc = ring(y, off), ring(x, off)
        total_a = hp[yc, x, :, 0:512].astype(F32)
        total_b = hp[y, xc, :, 512:1024].astype(F32)
        for k in range(3):
            total_a += ra[k, yc].astype(F32)
            total_b += rb[k, xc].astype(F32)
        if off == 0:
            g_own[:, 0:512] = total_a
            g_own[:, 512:1024] = total_b
        else:
            k = OFFSETS.index(off)
            ha[k] = total_a.astype(BF16)
            hb[k] = total_b.astype(BF16)
            second_a.send(ha.at[k], ra2.at[k], dev("y", off))
            second_b.send(hb.at[k], rb2.at[k], dev("x", off))

    put = []
    for n, (keep, out) in enumerate(((gk_ref, gw_hbm), (uk_ref, uw_hbm))):
        pair[n].wait_recv()

        def sum_step(j, _, n=n, keep=keep):
            cols = pl.ds(pl.multiple_of(j * 128, 128), 128)
            for i in range(2):
                rows = slice(i * 128, (i + 1) * 128)
                total = w_send[n, rows, cols].astype(F32) + w_recv[n, rows, cols].astype(F32)
                w_out_v[n, rows, cols] = (total * keep[i, j].astype(F32)).astype(BF16)
            return 0

        lax.fori_loop(0, HID // 128, sum_step, 0)
        put.append(fetch(9 + n, w_out_v.at[n], out))

    second_a.wait_recv()
    second_b.wait_recv()
    for h in range(HEADS):
        cols = slice(h * HD, (h + 1) * HD)
        total = g_own[:, cols]
        buf = ra2 if h < 4 else rb2
        low = slice((h % 4) * HD, (h % 4 + 1) * HD)
        for k in range(3):
            total += buf[k, :, low].astype(F32)
        g_s[h * ROWS : (h + 1) * ROWS, :] = total.astype(BF16)

    val1, val2 = Group(vt_r), Group(vt2_r)
    key1, key2 = Group(kt_r), Group(kt2_r)
    delta = jnp.sum(out_t[...] * g_s[...].astype(F32).T, axis=0, keepdims=True)
    for off in (2, -1, 1, 0):
        yc = ring(y, off)
        rows = pl.ds(pl.multiple_of(yc * 320, 320), 320)
        prob_grad = nt(v_all[yc].reshape(320, HD), g_s[...])
        part = nn(p_low[rows, :], g_s[...]).astype(BF16)
        for i in range(4):
            vt_s[yc, i] = part[i * ROWS : (i + 1) * ROWS, :]
        if off != 0:
            val1.send(vt_s.at[yc], vt_r.at[OFFSETS.index(off)], dev("y", off))
        score = (p_f[rows, :] * (prob_grad - delta) * SCALE).astype(BF16)
        ds_s[rows, :] = score
        part = nn(score, q_s[...]).astype(BF16)
        for i in range(4):
            kt_s[yc, i] = part[i * ROWS : (i + 1) * ROWS, :]
        for k, o in enumerate(OFFSETS):
            xc = ring(x, o)
            key1.send(kt_s.at[yc, xc], kt_r.at[k, yc], dev("x", o))

    def q_step(t, _):
        cols = pl.ds(pl.multiple_of(t * 128, 128), 128)
        q_s[cols, :] = nn(k_t[...], ds_s[:, cols]).T.astype(BF16)
        return 0

    lax.fori_loop(0, QS // 128, q_step, 0)
    for h in range(HEADS):
        dq_ref[0, :, h * HD : (h + 1) * HD] = q_s[h * ROWS : (h + 1) * ROWS, :]

    def add_up(first, own, recv, buf, axis, keep_at, second, landing):
        first.wait_recv()
        for k, o in enumerate(OFFSETS):
            spot = ring(keep_at, o)
            total = own(spot).astype(F32)
            for j in range(3):
                total += recv[j, spot].astype(F32)
            buf[k] = total.astype(BF16)
            second.send(buf.at[k], landing.at[k], dev(axis, o))
        total = own(keep_at).astype(F32)
        for j in range(3):
            total += recv[j, keep_at].astype(F32)
        return total

    val_own = add_up(val1, lambda i: vt_s[y, i], vt_r, vt2_s, "x", x, val2, vt2_r)
    key_own = add_up(key1, lambda i: kt_s[i, x], kt_r, kt2_s, "y", y, key2, kt2_r)
    for own, second, landing, out in (
        (val_own, val2, vt2_r, dv_ref),
        (key_own, key2, kt2_r, dk_ref),
    ):
        second.wait_recv()
        for k in range(3):
            own += landing[k].astype(F32)
        out[0] = own.astype(BF16)

    for group in groups:
        group.wait_send()
    for copy in put:
        copy.wait()


def hand_on(*refs):
    sources, targets, through, (get_sem, put_sem) = refs[:5], refs[5:10], refs[10:15], refs[15:]
    parts = []
    for n in range(5):
        for i in range(PARTS if n < 2 else 1):
            rows = pl.ds(i * (FEAT // PARTS), FEAT // PARTS) if n < 2 else 0
            parts.append([ref.at[rows] for ref in (sources[n], through[n], targets[n])])
    gets = [
        pltpu.make_async_copy(part[0], part[1], get_sem.at[i]) for i, part in enumerate(parts)
    ]
    puts = [
        pltpu.make_async_copy(part[1], part[2], put_sem.at[i]) for i, part in enumerate(parts)
    ]
    for get in gets:
        get.start()
    for get, put in zip(gets, puts):
        get.wait()
        put.start()
    for put in puts:
        put.wait()


def on_device(
    ffn_input,
    gate_act,
    up_act,
    hidden_grad,
    stream_grad,
    w_gate,
    w_up,
    gate_keep,
    up_keep,
    w_out,
    queries,
    keys,
    values,
):
    hbm = pl.BlockSpec(memory_space=pl.ANY)
    vmem = pl.BlockSpec(memory_space=pltpu.VMEM)
    smem = pl.BlockSpec(memory_space=pltpu.SMEM)
    chunk_grid = (4, 4, ROWS)
    out_shape = (
        jax.ShapeDtypeStruct((FEAT, HID), BF16),
        jax.ShapeDtypeStruct((FEAT, HID), BF16),
        jax.ShapeDtypeStruct((1, ROWS, HEADS * HD), BF16),
        jax.ShapeDtypeStruct((1, ROWS, HD), BF16),
        jax.ShapeDtypeStruct((1, ROWS, HD), BF16),
    )
    results = pl.pallas_call(
        kernel,
        out_shape=out_shape,
        in_specs=[hbm, vmem, vmem, vmem, hbm, hbm, hbm, smem, smem, hbm, hbm, vmem, vmem],
        out_specs=(hbm, hbm, vmem, vmem, vmem),
        scratch_shapes=[
            pltpu.VMEM(chunk_grid + (HID,), BF16),
            pltpu.VMEM(chunk_grid + (HID,), BF16),
            pltpu.VMEM(chunk_grid + (HD,), BF16),
            pltpu.VMEM(chunk_grid + (HD,), BF16),
            pltpu.VMEM((2, FEAT, HID), BF16),
            pltpu.VMEM((SEQ, FEAT), BF16),
            pltpu.VMEM((FEAT, SEQ), BF16),
            pltpu.VMEM((HEADS * HD, FEAT), BF16),
            pltpu.VMEM((ROWS, HEADS * HD), BF16),
            pltpu.VMEM((QS, HD), BF16),
            pltpu.VMEM((4, ROWS, HD), BF16),
            pltpu.VMEM((4, 8, ROWS, HD), BF16),
            pltpu.VMEM((4, 7, ROWS, HD), BF16),
            pltpu.VMEM((4, 4, 2, ROWS, HD), BF16),
            pltpu.VMEM(chunk_grid + (HEADS * HD,), BF16),
            pltpu.VMEM((3, 4, ROWS, 512), BF16),
            pltpu.VMEM((3, 4, ROWS, 512), BF16),
            pltpu.VMEM((3, ROWS, 512), BF16),
            pltpu.VMEM((3, ROWS, 512), BF16),
            pltpu.VMEM((3, ROWS, 512), BF16),
            pltpu.VMEM((3, ROWS, 512), BF16),
            pltpu.VMEM((ROWS, HEADS * HD), F32),
            pltpu.VMEM((QS, HD), BF16),
            pltpu.VMEM((2, FEAT, HID), BF16),
            pltpu.VMEM((2, FEAT, HID), BF16),
            pltpu.VMEM((2, FEAT, HID), BF16),
            pltpu.VMEM((HD, SEQ), BF16),
            pltpu.VMEM((HD, SEQ), BF16),
            pltpu.VMEM((HD, QS), F32),
            pltpu.VMEM((SEQ, QS), F32),
            pltpu.VMEM((SEQ, QS), BF16),
            pltpu.VMEM((SEQ, QS), BF16),
            pltpu.VMEM(chunk_grid + (HD,), BF16),
            pltpu.VMEM(chunk_grid + (HD,), BF16),
            pltpu.VMEM((3, 4, ROWS, HD), BF16),
            pltpu.VMEM((3, 4, ROWS, HD), BF16),
            pltpu.VMEM((3, ROWS, HD), BF16),
            pltpu.VMEM((3, ROWS, HD), BF16),
            pltpu.VMEM((3, ROWS, HD), BF16),
            pltpu.VMEM((3, ROWS, HD), BF16),
            pltpu.SemaphoreType.DMA((N_GROUPS,)),
            pltpu.SemaphoreType.DMA((N_GROUPS,)),
            pltpu.SemaphoreType.DMA((11,)),
        ],
        compiler_params=pltpu.CompilerParams(
            collective_id=0, has_side_effects=True, vmem_limit_bytes=56 * 1024 * 1024
        ),
    )(
        ffn_input,
        gate_act,
        up_act,
        hidden_grad,
        stream_grad.reshape(16, ROWS, FEAT),
        w_gate,
        w_up,
        gate_keep,
        up_keep,
        w_out,
        queries,
        keys,
        values,
    )
    return pl.pallas_call(
        hand_on,
        out_shape=out_shape,
        in_specs=[hbm] * 5,
        out_specs=(hbm,) * 5,
        scratch_shapes=[pltpu.VMEM(shape.shape, BF16) for shape in out_shape]
        + [pltpu.SemaphoreType.DMA((2 * PARTS + 3,))] * 2,
        compiler_params=pltpu.CompilerParams(vmem_limit_bytes=60 * 1024 * 1024),
    )(*results)


def solution(mesh):
    placed = (
        P("dp", None, "row"),
        P("dp", "row", "col"),
        P("dp", "row", "col"),
        P("dp", "row", "col"),
        P("dp", None, "row"),
        P("row", "col"),
        P("row", "col"),
        P("row", "col"),
        P("row", "col"),
        P("col", "row"),
        P("dp", "row", "col"),
        P("dp", "row", "col"),
        P("dp", "row", "col"),
    )
    return jax.shard_map(
        on_device,
        mesh=mesh,
        in_specs=placed,
        out_specs=(
            P("row", "col"),
            P("row", "col"),
            P("dp", "row", "col"),
            P("dp", "row", "col"),
            P("dp", "row", "col"),
        ),
        check_vma=False,
    )
```
